128 devices in a mesh: atoms: 64 (over y_hi, x, z, core), dirs: 2 (over y_lo).
Axes of the slice: x: 4, y: 4 (y_hi: 2, y_lo: 2; y = y_hi * 2 + y_lo), z: 4, core: 2. Of those that a mesh axis runs over, the one named last changes fastest.
Arguments:
- queries: bfloat16 [131072, 128], P('atoms'), may hold values from -6 to 6
- keys: bfloat16 [131072, 128], P('atoms'), may hold values from -6 to 6
- values: bfloat16 [131072, 128], P('atoms'), may hold values from -6 to 6
- cotangent: bfloat16 [131072, 128], P('atoms'), may hold values from -6 to 6
- positions: float32 [3, 131072], P(None, 'atoms'), may hold values from -128 to 128
- species: int32 [131072], P('atoms'), may hold values from 0 to 4
- domain: int32 [131072], P('atoms'), may hold values from 0 to 64, as said below
- species_gain: float32 [5, 128], replicated, may hold values from 0.1 to 1.9
- frequency: float32 [32], replicated, may hold values from 0.02 to 1
- directions: float32 [3, 88], P(None, 'dirs'), may hold values from -1 to 1, as said below
- dir_weight: float32 [88], P('dirs'), may hold values from 0.003 to 0.03
- dir_mask: int32 [88], P('dirs'), may hold values from 0 to 1, as said below
Outputs:
- attended: bfloat16 [131072, 128], P(('atoms', 'dirs'))
- grad_queries: bfloat16 [131072, 128], P(('atoms', 'dirs'))
- grad_keys: bfloat16 [131072, 128], P(('atoms', 'dirs'))
- grad_values: bfloat16 [131072, 128], P(('atoms', 'dirs'))
The draws below stay inside these ranges and needn't reach their ends.
Inputs may be any that keep to these rules, and one draw needn't show every extreme that they name: The 2048 slots from b * 2048 on belong to domain b: they hold b for its atoms first, then 131072 // 2048 for empty slots; every domain has 1024 to 2048 atoms. `directions`: each column is a unit vector. `dir_mask`: exactly 86 entries are 1.
All inputs are finite; a program needn't handle non-finite values.
Results may differ from the reference program's by a relative error of at most 0.012.
Values may be sent and summed in bfloat16 or wider, within the bound.
A program may use at most 128 MiB of HBM per device.

```python
import math
import jax
import jax.numpy as jnp
from jax import lax

F = 128
FREQS = 32
DIRS = 88
SPECIES = 5
ATOMS_DEV = 2048
ATOMS = 131072


def draw_domain(key, part):
    key = jax.random.fold_in(key, 7)
    domain_count = ATOMS // ATOMS_DEV
    count_key, pick_key = jax.random.split(key)
    filled = jax.random.randint(count_key, (domain_count,), ATOMS_DEV // 2, ATOMS_DEV + 1)
    picked = jax.random.permutation(pick_key, domain_count)
    filled = jnp.where(picked == 0, ATOMS_DEV, filled)
    filled = jnp.where(picked == 1, ATOMS_DEV // 2, filled)
    slot_index = jnp.arange(ATOMS, dtype=jnp.int32)
    owner = slot_index // ATOMS_DEV
    within = slot_index % ATOMS_DEV
    return jnp.where(within < filled[owner], owner, domain_count).astype(jnp.int32)


def draw_positions(key, part):
    key = jax.random.fold_in(key, 11)
    along_key, side_key = jax.random.split(key)
    domain_count = ATOMS // ATOMS_DEV
    owner = (jnp.arange(ATOMS, dtype=jnp.int32) // ATOMS_DEV).astype(jnp.float32)
    offset = jax.random.uniform(along_key, (ATOMS,), jnp.float32)
    along = (owner + offset) * 4.0 - 2.0 * domain_count
    across = jax.random.uniform(side_key, (2, ATOMS), jnp.float32, -16.0, 16.0)
    return jnp.concatenate([along[None, :], across], axis=0)


def draw_directions(key, part):
    key = jax.random.fold_in(key, 13)
    raw_vectors = jax.random.normal(key, (3, DIRS), jnp.float32)
    return raw_vectors / jnp.sqrt(jnp.sum(raw_vectors * raw_vectors, axis=0, keepdims=True) + 1e-06)


def draw_dir_mask(key, part):
    key = jax.random.fold_in(key, 17)
    ordering = jax.random.permutation(key, DIRS)
    return (ordering < DIRS - 2).astype(jnp.int32)


def place_ends(entries, stream_key, least, top_value):
    longest = entries.shape.index(max(entries.shape))
    spots = []
    for shift in (0, 1):
        where = [jax.random.randint(jax.random.fold_in(stream_key, axis), (), 0, length) for axis, length in enumerate(entries.shape)]
        where[longest] = (where[longest] + shift) % entries.shape[longest]
        spots.append(tuple(where))
    return entries.at[spots[0]].set(least).at[spots[1]].set(top_value)


def shard_levels(rng, dims, shards, smallest, largest):
    def one(axis_at, shards_of):
        draws = jax.random.uniform(jax.random.fold_in(jax.random.fold_in(rng, 6), axis_at), (shards_of,), jnp.float32, smallest / len(shards), largest / len(shards))
        return jnp.repeat(jnp.exp(draws), dims[axis_at] // shards_of).reshape((-1,) + (1,) * (len(dims) - axis_at - 1))

    factor_of = one(*shards[0])
    for cut in shards[1:]:
        factor_of = factor_of * one(*cut)
    return factor_of


def centred(own_key, extent, scale, bound, pieces=(), kind=jnp.bfloat16):
    entries = scale * jax.random.normal(own_key, extent, jnp.float32)
    if pieces:
        entries = entries * shard_levels(own_key, extent, pieces, -0.22, 0.18)
    return jnp.clip(entries, -bound, bound).astype(kind)


def setup_inputs(seed: int = 0) -> dict:
    seeds = jax.random.split(jax.random.key(seed), 13)
    queries = centred(seeds[0], (ATOMS, F), 1.0, 6.0, ((0, 64),))
    keys = centred(seeds[1], (ATOMS, F), 1.0, 6.0, ((0, 64),))
    values = centred(seeds[2], (ATOMS, F), 1.0, 6.0, ((0, 64),))
    cotangent = centred(seeds[3], (ATOMS, F), 1.0, 6.0, ((0, 64),))
    positions = draw_positions(jax.random.fold_in(seeds[12], 71), 0)
    species = place_ends(jax.random.randint(seeds[5], (ATOMS,), 0, SPECIES), jax.random.fold_in(seeds[5], 1), 0, SPECIES - 1).astype(jnp.int32)
    domain = draw_domain(jax.random.fold_in(seeds[12], 71), 0)
    species_gain = jnp.clip(1.0 + 0.18 * jax.random.normal(seeds[7], (SPECIES, F), jnp.float32), 0.1, 1.9)
    frequency = jnp.clip(jnp.exp(jax.random.uniform(seeds[8], (FREQS,), jnp.float32, math.log(0.02), math.log(1.0))), 0.02, 1.0)
    directions = draw_directions(jax.random.fold_in(seeds[12], 71), 0)
    dir_weight = jnp.clip(jnp.exp(math.log(0.03) - 2.3025851 * jax.random.uniform(seeds[10], (DIRS,), jnp.float32) ** shard_levels(seeds[10], (DIRS,), ((0, 2),), -0.2, 0.2)), 0.003, 0.03)
    dir_mask = draw_dir_mask(jax.random.fold_in(seeds[12], 71), 0)
    return dict(queries=queries, keys=keys, values=values, cotangent=cotangent, positions=positions, species=species, domain=domain, species_gain=species_gain, frequency=frequency, directions=directions, dir_weight=dir_weight, dir_mask=dir_mask)


def rotate(features, cosine, sine_val):
    half_width = features.shape[-1] // 2
    leading = features[..., :half_width]
    trailing = features[..., half_width:]
    return jnp.concatenate([leading * cosine - trailing * sine_val, leading * sine_val + trailing * cosine], axis=-1)

def rounded(matrix):
    return lax.optimization_barrier(matrix.astype(jnp.bfloat16)).astype(jnp.float32)

def reference(queries, keys, values, cotangent, positions, species, domain, species_gain, frequency, directions, dir_weight, dir_mask):
    slot_owner = (jnp.arange(ATOMS, dtype=jnp.int32) // ATOMS_DEV).astype(jnp.int32)
    alive_mask = (domain == slot_owner).astype(jnp.float32)[:, None]
    gain_rows = species_gain[species]
    keys_gained = keys.astype(jnp.float32) * gain_rows * alive_mask
    queries_full = queries.astype(jnp.float32)
    values_live = values.astype(jnp.float32) * alive_mask
    grad_live = cotangent.astype(jnp.float32) * alive_mask
    dir_coef = dir_weight * dir_mask.astype(jnp.float32) / math.sqrt(F * ATOMS_DEV)
    pair_freq = jnp.tile(frequency, F // 2 // FREQS)
    projected = directions[0][:, None] * positions[0][None, :] + directions[1][:, None] * positions[1][None, :]
    projected = projected + directions[2][:, None] * positions[2][None, :]
    highest = lax.Precision.HIGHEST

    def direction_step(totals, inputs_step):
        out_total, query_total, key_total, value_total = totals
        dir_proj, dir_scale = inputs_step
        phase_angle = dir_proj[:, None] * pair_freq[None, :]
        cosine = jnp.cos(phase_angle)
        sine_val = jnp.sin(phase_angle)
        query_rot = rounded(rotate(queries_full, cosine, sine_val))
        key_rot = rounded(rotate(keys_gained, cosine, sine_val))
        state_full = jnp.dot(key_rot.T, values_live, precision=highest, preferred_element_type=jnp.float32)
        state_b = rounded(state_full)
        out_total = out_total + dir_scale * jnp.dot(query_rot, state_b, precision=highest, preferred_element_type=jnp.float32)
        back_query = dir_scale * jnp.dot(grad_live, state_b.T, precision=highest, preferred_element_type=jnp.float32)
        query_total = query_total + rotate(back_query, cosine, -sine_val)
        state_grad = rounded(dir_scale * jnp.dot(query_rot.T, grad_live, precision=highest, preferred_element_type=jnp.float32))
        back_key = jnp.dot(values_live, state_grad.T, precision=highest, preferred_element_type=jnp.float32)
        key_total = key_total + rotate(back_key, cosine, -sine_val)
        value_total = value_total + jnp.dot(key_rot, state_grad, precision=highest, preferred_element_type=jnp.float32)
        return ((out_total, query_total, key_total, value_total), None)
    zeros_full = jnp.zeros((ATOMS, F), jnp.float32)
    totals, _ = lax.scan(direction_step, (zeros_full, zeros_full, zeros_full, zeros_full), (projected, dir_coef))
    out_total, query_total, key_total, value_total = totals
    attended = (out_total * alive_mask).astype(jnp.bfloat16)
    grad_queries = query_total.astype(jnp.bfloat16)
    grad_keys = (key_total * gain_rows * alive_mask).astype(jnp.bfloat16)
    grad_values = value_total.astype(jnp.bfloat16)
    return (attended, grad_queries, grad_keys, grad_values)
```

```python
import functools
import math

import jax
import jax.numpy as jnp
from jax import lax
from jax.experimental import pallas as pl
from jax.experimental.pallas import tpu as pltpu
from jax.sharding import PartitionSpec as P

F32 = jnp.float32
BF16 = jnp.bfloat16

ATOMS = 2048
HALF = ATOMS // 2
FEAT = 128
FREQS = 32
DIRS = 44
GROUP = 4
STEPS = DIRS // GROUP
ROWS = GROUP * FEAT
WIDTH = 256

SINE = (
    4.442882919124345,
    -7.3082456865090855,
    3.606354218433185,
    -0.8461116503751638,
    0.10982451642692614,
)
COSINE = (
    1.4142134962552289,
    -6.978850948563847,
    5.739460376907657,
    -1.8835579059891776,
    0.3106880275307806,
)

CORE_RS, X_RS, Z_RS, Y_RS, Y_AG, Z_AG, X_AG, CORE_AG = 0, 1, 4, 7, 8, 9, 12, 15
MESSAGES = 16
LAGS = (0, 1, 3, 4, 5, 6, 7, 9, 10)


def horner(coefficients, square):
    total = square * coefficients[-1] + coefficients[-2]
    for coefficient in coefficients[-3::-1]:
        total = total * square + coefficient
    return total


def cos_sin_turns(turns):
    nearest = (turns + 12582912.0) - 12582912.0
    rest = turns - nearest
    square = rest * rest
    sine = horner(SINE, square) * rest
    cosine = horner(COSINE, square)
    return 1.0 - sine * sine, sine * cosine


def tile_of(start, size, unit):
    return pl.ds(pl.multiple_of(start, unit), size)


def kernel(
    freq_ref,
    dirs_ref,
    weight_ref,
    mask_ref,
    q_ref,
    k_ref,
    v_ref,
    g_ref,
    pos_ref,
    species_ref,
    domain_ref,
    gain_ref,
    att_out,
    gq_out,
    gk_out,
    gv_out,
    freq_tile,
    pos_tile,
    gain_tile,
    alive_tile,
    key_t,
    query_t,
    value_t,
    grad_t,
    cos_sin,
    key_rot,
    query_rot,
    back_q,
    back_k,
    att_acc,
    gv_acc,
    gq_acc,
    gk_acc,
    part,
    core_in,
    core_sum,
    x_in,
    x_sum,
    z_in,
    z_sum,
    y_in,
    state,
    out_send,
    out_recv,
    send_sem,
    recv_sem,
    out_send_sem,
    out_recv_sem,
):
    atoms_at = lax.axis_index("atoms")
    dirs_at = lax.axis_index("dirs")
    core = lax.rem(atoms_at, 2)
    z_at = lax.rem(lax.div(atoms_at, 2), 4)
    x_at = lax.rem(lax.div(atoms_at, 8), 4)
    y_at = lax.div(atoms_at, 32)

    def device(y, x, z, c):
        return {"atoms": ((y * 4 + x) * 4 + z) * 2 + c}

    other_core = device(y_at, x_at, z_at, 1 - core)
    other_y = device(1 - y_at, x_at, z_at, core)
    x_far = [lax.rem(x_at + d, 4) for d in range(4)]
    z_far = [lax.rem(z_at + d, 4) for d in range(4)]
    x_peers = [device(y_at, x_far[d], z_at, core) for d in range(4)]
    z_peers = [device(y_at, x_at, z_far[d], core) for d in range(4)]
    other_dirs = {"dirs": 1 - dirs_at}

    barrier = pltpu.get_barrier_semaphore()
    partners = [other_core, other_y, other_dirs] + x_peers[1:] + z_peers[1:]
    for partner in partners:
        pl.semaphore_signal(
            barrier, inc=1, device_id=partner, device_id_type=pl.DeviceIdType.MESH
        )

    core_row = core * ROWS
    x_row = core_row + x_at * FEAT
    z_row = x_row + z_at * 32
    y_row = z_row + y_at * 16

    def message(number, g):
        if number == CORE_RS:
            src = part.at[g, tile_of((1 - core) * ROWS, ROWS, ROWS)]
            dst, to = core_in.at[g], other_core
        elif number < Z_RS:
            d = number - X_RS + 1
            src = core_sum.at[g, tile_of(x_far[d] * FEAT, FEAT, FEAT)]
            dst, to = x_in.at[g, 3 - d], x_peers[d]
        elif number < Y_RS:
            d = number - Z_RS + 1
            src = x_sum.at[g, tile_of(z_far[d] * 32, 32, 32)]
            dst, to = z_in.at[g, 3 - d], z_peers[d]
        elif number == Y_RS:
            src = z_sum.at[g, tile_of((1 - y_at) * 16, 16, 16)]
            dst, to = y_in.at[g], other_y
        elif number == Y_AG:
            src = dst = state.at[g, tile_of(y_row, 16, 16)]
            to = other_y
        elif number < X_AG:
            src = dst = state.at[g, tile_of(z_row, 32, 32)]
            to = z_peers[number - Z_AG + 1]
        elif number < CORE_AG:
            src = dst = state.at[g, tile_of(x_row, FEAT, FEAT)]
            to = x_peers[number - X_AG + 1]
        else:
            src = dst = state.at[g, tile_of(core_row, ROWS, ROWS)]
            to = other_core
        return pltpu.make_async_remote_copy(
            src_ref=src,
            dst_ref=dst,
            send_sem=send_sem.at[number, g],
            recv_sem=recv_sem.at[number, g],
            device_id=to,
            device_id_type=pl.DeviceIdType.MESH,
        )

    def send(first, count, g):
        for number in range(first, first + count):
            message(number, g).start()

    def receive(first, count, g):
        for number in range(first, first + count):
            message(number, g).wait()

    def stage_0(g):
        send(CORE_RS, 1, g)

    def stage_1(g):
        receive(CORE_RS, 1, g)
        mine = part[g, tile_of(core_row, ROWS, ROWS), :].astype(F32)
        core_sum[g] = (mine + core_in[g].astype(F32)).astype(BF16)
        send(X_RS, 3, g)

    def stage_2(g):
        receive(X_RS, 3, g)
        total = core_sum[g, tile_of(x_at * FEAT, FEAT, FEAT), :].astype(F32)
        for slot in range(3):
            total = total + x_in[g, slot].astype(F32)
        x_sum[g] = total
        send(Z_RS, 3, g)

    def stage_3(g):
        receive(Z_RS, 3, g)
        total = x_sum[g, tile_of(z_at * 32, 32, 32), :]
        for slot in range(3):
            total = total + z_in[g, slot]
        z_sum[g] = total
        send(Y_RS, 1, g)

    def stage_4(g):
        receive(Y_RS, 1, g)
        total = z_sum[g, tile_of(y_at * 16, 16, 16), :] + y_in[g]
        state[g, tile_of(y_row, 16, 16), :] = total.astype(BF16)
        send(Y_AG, 1, g)

    def stage_5(g):
        receive(Y_AG, 1, g)
        send(Z_AG, 3, g)

    def stage_6(g):
        receive(Z_AG, 3, g)
        send(X_AG, 3, g)

    def stage_7(g):
        receive(X_AG, 3, g)
        send(CORE_AG, 1, g)

    def stage_8(g):
        receive(CORE_AG, 1, g)

    stages = (stage_0, stage_1, stage_2, stage_3, stage_4, stage_5, stage_6, stage_7, stage_8)

    def exchange(t, lowest, highest):
        for number in range(len(stages) - 1, -1, -1):
            lag = LAGS[number]
            if highest < lag or lowest - lag >= STEPS:
                continue
            if lowest >= lag and highest - lag < STEPS:
                stages[number](t - lag)
            else:

                @pl.when(jnp.logical_and(t >= lag, t < lag + STEPS))
                def _(number=number, lag=lag):
                    stages[number](t - lag)

    for f in range(FREQS):
        freq_tile[f : f + 1, :] = jnp.full((1, 128), freq_ref[f] * (0.5 / math.pi), F32)
    for axis in range(3):
        pos_tile[axis] = jnp.broadcast_to(pos_ref[axis : axis + 1, :], (8, ATOMS))
    for s in range(gain_ref.shape[0]):
        gain_tile[s] = jnp.broadcast_to(gain_ref[s : s + 1, :], (FEAT, FEAT)).T
    alive_tile[...] = jnp.broadcast_to(
        jnp.where(domain_ref[...] == atoms_at, 1.0, 0.0), (8, ATOMS)
    )

    def alive_of(columns):
        return jnp.concatenate([alive_tile[:, columns]] * (FEAT // 8), axis=0)

    def gain_of(columns):
        species = jnp.broadcast_to(species_ref[:, columns], (FEAT, 128))
        gain = gain_tile[0]
        for s in range(1, gain_ref.shape[0]):
            gain = jnp.where(species == s, gain_tile[s], gain)
        return gain * alive_of(columns)

    def prepare(block, carry):
        columns = tile_of(block * 128, 128, 128)
        key_t[:, columns] = (k_ref[columns, :].astype(F32).T * gain_of(columns)).astype(BF16)
        query_t[:, columns] = (q_ref[columns, :].astype(F32).T * alive_of(columns)).astype(BF16)
        value_t[:, columns] = v_ref[columns, :].astype(F32).T.astype(BF16)
        grad_t[:, columns] = g_ref[columns, :].astype(F32).T.astype(BF16)
        return carry

    lax.fori_loop(0, ATOMS // 128, prepare, 0)

    def coef(u):
        return weight_ref[u] * mask_ref[u].astype(F32) * (1.0 / math.sqrt(FEAT * ATOMS))

    def rotate_to(x_ref, y_ref, u, p, columns, place, cosine, sine):
        lead = x_ref[p : p + 16, columns]
        trail = x_ref[p + 64 : p + 80, columns]
        y_ref[u, p : p + 16, place] = lead * cosine - trail * sine
        y_ref[u, p + 64 : p + 80, place] = lead * sine + trail * cosine

    def state_step(i):
        for u in range(GROUP):
            at = i * GROUP + u
            for low in range(0, ATOMS, WIDTH):
                columns = pl.ds(low, WIDTH)
                projected = (
                    dirs_ref[0, at] * pos_tile[0, :, columns]
                    + dirs_ref[1, at] * pos_tile[1, :, columns]
                    + dirs_ref[2, at] * pos_tile[2, :, columns]
                )
                for low_f in range(0, FREQS, 16):
                    pairs = []
                    for f in (low_f, low_f + 8):
                        freq = jnp.concatenate([freq_tile[f : f + 8, :]] * (WIDTH // 128), axis=1)
                        pairs.append(cos_sin_turns(projected * freq))
                    cosine = jnp.concatenate([pairs[0][0], pairs[1][0]], axis=0).astype(BF16)
                    sine = jnp.concatenate([pairs[0][1], pairs[1][1]], axis=0).astype(BF16)
                    cos_sin[at, 0, low_f : low_f + 16, columns] = cosine
                    cos_sin[at, 1, low_f : low_f + 16, columns] = sine
                    for p in (low_f, low_f + FREQS):
                        rotate_to(key_t, key_rot, u, p, columns, columns, cosine, sine)
                        rotate_to(query_t, query_rot, u, p, columns, columns, cosine, sine)
        for at_row, rotated, rows in ((0, key_rot, v_ref), (ROWS, query_rot, g_ref)):
            product = jnp.dot(
                rotated[...].reshape(ROWS, ATOMS), rows[...], preferred_element_type=F32
            )
            for u in range(GROUP):
                part[i, at_row + u * FEAT : at_row + (u + 1) * FEAT, :] = (
                    product[u * FEAT : (u + 1) * FEAT] * coef(i * GROUP + u)
                ).astype(BF16)

    def output_step(i, base):
        for u in range(GROUP):
            at = i * GROUP + u
            for low in range(0, HALF, WIDTH):
                place = pl.ds(low, WIDTH)
                columns = tile_of(base + low, WIDTH, WIDTH)
                for low_f in range(0, FREQS, 16):
                    cosine = cos_sin[at, 0, low_f : low_f + 16, columns]
                    sine = cos_sin[at, 1, low_f : low_f + 16, columns]
                    for p in (low_f, low_f + FREQS):
                        rotate_to(key_t, key_rot, u, p, columns, place, cosine, sine)
                        rotate_to(query_t, query_rot, u, p, columns, place, cosine, sine)
        columns = tile_of(base, HALF, HALF)
        forward = state[i, :ROWS, :]
        backward = state[i, ROWS:, :]
        contract = (((0,), (0,)), ((), ()))
        for matrix, rotated, rows_t, total, back in (
            (forward, query_rot, grad_t, att_acc, back_q),
            (backward, key_rot, value_t, gv_acc, back_k),
        ):
            back[...] = (
                jnp.dot(matrix, rows_t[:, columns], preferred_element_type=F32)
                .astype(BF16)
                .reshape(GROUP, FEAT, HALF)
            )
            total[...] += lax.dot_general(
                matrix,
                rotated[:, :, :HALF].reshape(ROWS, HALF),
                contract,
                preferred_element_type=F32,
            )
        for low in range(0, HALF, WIDTH):
            place = pl.ds(low, WIDTH)
            columns = tile_of(base + low, WIDTH, WIDTH)
            for low_f in range(0, FREQS, 16):
                cosines = [
                    cos_sin[i * GROUP + u, 0, low_f : low_f + 16, columns] for u in range(GROUP)
                ]
                sines = [
                    cos_sin[i * GROUP + u, 1, low_f : low_f + 16, columns] for u in range(GROUP)
                ]
                for p in (low_f, low_f + FREQS):
                    for back, total in ((back_q, gq_acc), (back_k, gk_acc)):
                        lead_sum = trail_sum = None
                        for u in range(GROUP):
                            lead = back[u, p : p + 16, place]
                            trail = back[u, p + 64 : p + 80, place]
                            new_lead = lead * cosines[u] + trail * sines[u]
                            new_trail = trail * cosines[u] - lead * sines[u]
                            lead_sum = new_lead if u == 0 else lead_sum + new_lead
                            trail_sum = new_trail if u == 0 else trail_sum + new_trail
                        total[p : p + 16, place] += lead_sum.astype(F32)
                        total[p + 64 : p + 80, place] += trail_sum.astype(F32)

    totals = (att_acc, gq_acc, gk_acc, gv_acc)

    def clear():
        for total in totals:
            total[...] = jnp.zeros_like(total)

    pl.semaphore_wait(barrier, len(partners))

    def first_loop(t, carry):
        state_step(t)
        exchange(t, 0, STEPS - 1)
        return carry

    lax.fori_loop(0, STEPS, first_loop, 0)

    clear()
    far_base = (1 - dirs_at) * HALF

    def second_loop(i, carry):
        exchange(i + STEPS, STEPS, 2 * STEPS - 1)
        output_step(i, far_base)
        return carry

    lax.fori_loop(0, STEPS, second_loop, 0)

    def out_message(n):
        return pltpu.make_async_remote_copy(
            src_ref=out_send.at[n],
            dst_ref=out_recv.at[n],
            send_sem=out_send_sem.at[n],
            recv_sem=out_recv_sem.at[n],
            device_id=other_dirs,
            device_id_type=pl.DeviceIdType.MESH,
        )

    for n, total in enumerate(totals):
        out_send[n] = total[...].astype(BF16)
        out_message(n).start()
    clear()
    near_base = dirs_at * HALF

    def third_loop(i, carry):
        output_step(i, near_base)
        return carry

    lax.fori_loop(0, STEPS, third_loop, 0)

    for n in range(4):
        out_message(n).wait()

    def finish(block, carry):
        place = tile_of(block * 128, 128, 128)
        columns = tile_of(near_base + block * 128, 128, 128)
        alive = alive_of(columns)
        for n, (total, out, factor) in enumerate(
            zip(
                totals,
                (att_out, gq_out, gk_out, gv_out),
                (None, alive, gain_of(columns), None),
            )
        ):
            whole = total[:, place] + out_recv[n, :, place].astype(F32)
            if factor is not None:
                whole = whole * factor
            out[place, :] = whole.T.astype(BF16)
        return carry

    lax.fori_loop(0, HALF // 128, finish, 0)


def per_device(
    queries,
    keys,
    values,
    cotangent,
    positions,
    species,
    domain,
    species_gain,
    frequency,
    directions,
    dir_weight,
    dir_mask,
):
    smem = pl.BlockSpec(memory_space=pltpu.SMEM)
    vmem = pl.BlockSpec(memory_space=pltpu.VMEM)
    species_count = species_gain.shape[0]
    scratch = [
        pltpu.VMEM((FREQS, 128), F32),
        pltpu.VMEM((3, 8, ATOMS), F32),
        pltpu.VMEM((species_count, FEAT, FEAT), F32),
        pltpu.VMEM((8, ATOMS), F32),
        pltpu.VMEM((FEAT, ATOMS), BF16),
        pltpu.VMEM((FEAT, ATOMS), BF16),
        pltpu.VMEM((FEAT, ATOMS), BF16),
        pltpu.VMEM((FEAT, ATOMS), BF16),
        pltpu.VMEM((DIRS, 2, FREQS, ATOMS), BF16),
        pltpu.VMEM((GROUP, FEAT, ATOMS), BF16),
        pltpu.VMEM((GROUP, FEAT, ATOMS), BF16),
        pltpu.VMEM((GROUP, FEAT, HALF), BF16),
        pltpu.VMEM((GROUP, FEAT, HALF), BF16),
        pltpu.VMEM((FEAT, HALF), F32),
        pltpu.VMEM((FEAT, HALF), F32),
        pltpu.VMEM((FEAT, HALF), F32),
        pltpu.VMEM((FEAT, HALF), F32),
        pltpu.VMEM((STEPS, 2 * ROWS, FEAT), BF16),
        pltpu.VMEM((STEPS, ROWS, FEAT), BF16),
        pltpu.VMEM((STEPS, ROWS, FEAT), BF16),
        pltpu.VMEM((STEPS, 3, FEAT, FEAT), BF16),
        pltpu.VMEM((STEPS, FEAT, FEAT), F32),
        pltpu.VMEM((STEPS, 3, 32, FEAT), F32),
        pltpu.VMEM((STEPS, 32, FEAT), F32),
        pltpu.VMEM((STEPS, 16, FEAT), F32),
        pltpu.VMEM((STEPS, 2 * ROWS, FEAT), BF16),
        pltpu.VMEM((4, FEAT, HALF), BF16),
        pltpu.VMEM((4, FEAT, HALF), BF16),
        pltpu.SemaphoreType.DMA((MESSAGES, STEPS)),
        pltpu.SemaphoreType.DMA((MESSAGES, STEPS)),
        pltpu.SemaphoreType.DMA((4,)),
        pltpu.SemaphoreType.DMA((4,)),
    ]
    att, gq, gk, gv = pl.pallas_call(
        kernel,
        out_shape=[jax.ShapeDtypeStruct((HALF, FEAT), BF16)] * 4,
        in_specs=[smem] * 4 + [vmem] * 8,
        out_specs=[vmem] * 4,
        scratch_shapes=scratch,
        compiler_params=pltpu.CompilerParams(
            collective_id=0, has_side_effects=True, vmem_limit_bytes=56 * 2**20
        ),
        name="fast_attention",
    )(
        frequency,
        directions,
        dir_weight,
        dir_mask,
        queries,
        keys,
        values,
        cotangent,
        positions,
        species.reshape(1, ATOMS),
        domain.reshape(1, ATOMS),
        species_gain,
    )
    return att, gq, gk, gv


def solution(mesh):
    return jax.shard_map(
        per_device,
        mesh=mesh,
        in_specs=(
            P("atoms", None),
            P("atoms", None),
            P("atoms", None),
            P("atoms", None),
            P(None, "atoms"),
            P("atoms"),
            P("atoms"),
            P(),
            P(),
            P(None, "dirs"),
            P("dirs"),
            P("dirs"),
        ),
        out_specs=(
            P(("atoms", "dirs"), None),
            P(("atoms", "dirs"), None),
            P(("atoms", "dirs"), None),
            P(("atoms", "dirs"), None),
        ),
        check_vma=False,
    )
```

```python
import functools
import math

import jax
import jax.numpy as jnp
from jax import lax
from jax.experimental import pallas as pl
from jax.experimental.pallas import tpu as pltpu
from jax.sharding import PartitionSpec as P

F32 = jnp.float32
BF16 = jnp.bfloat16

ATOMS = 2048
HALF = ATOMS // 2
FEAT = 128
FREQS = 32
DIRS = 44
GROUP = 4
STEPS = DIRS // GROUP
ROWS = GROUP * FEAT
WIDTH = 256

SINE = (
    4.442882919124345,
    -7.3082456865090855,
    3.606354218433185,
    -0.8461116503751638,
    0.10982451642692614,
)
COSINE = (
    1.4142134962552289,
    -6.978850948563847,
    5.739460376907657,
    -1.8835579059891776,
    0.3106880275307806,
)

CORE_RS, RING_RS, HOP_RS, LINE_RS, Y_RS = 0, 1, 3, 5, 8
Y_AG, LINE_AG, RING_AG, HOP_AG, CORE_AG = 9, 12, 15, 17, 19
MESSAGES = 20
STAGES = 11


def horner(coefficients, square):
    total = square * coefficients[-1] + coefficients[-2]
    for coefficient in coefficients[-3::-1]:
        total = total * square + coefficient
    return total


def cos_sin_turns(turns):
    nearest = (turns + 12582912.0) - 12582912.0
    rest = turns - nearest
    square = rest * rest
    sine = horner(SINE, square) * rest
    cosine = horner(COSINE, square)
    return 1.0 - sine * sine, sine * cosine


def tile_of(start, size, unit):
    return pl.ds(pl.multiple_of(start, unit), size)


def kernel(
    freq_ref,
    dirs_ref,
    weight_ref,
    mask_ref,
    dirs_rows_ref,
    q_ref,
    k_ref,
    v_ref,
    g_ref,
    pos_ref,
    species_ref,
    domain_ref,
    gain_ref,
    att_out,
    gq_out,
    gk_out,
    gv_out,
    freq_tile,
    pos_tile,
    gain_tile,
    alive_tile,
    key_t,
    query_t,
    value_t,
    grad_t,
    cos_sin,
    far_cos_sin,
    key_rot,
    query_rot,
    back_q,
    back_k,
    att_acc,
    gv_acc,
    gq_acc,
    gk_acc,
    part,
    core_in,
    core_sum,
    ring_in,
    relay,
    hop_in,
    line_sum,
    line_in,
    y_sum,
    y_in,
    state,
    dirs_send,
    dirs_recv,
    far_dirs,
    send_sem,
    recv_sem,
    dirs_sem,
):
    atoms_at = lax.axis_index("atoms")
    dirs_at = lax.axis_index("dirs")
    core = lax.rem(atoms_at, 2)
    z_at = lax.rem(lax.div(atoms_at, 2), 4)
    x_at = lax.rem(lax.div(atoms_at, 8), 4)
    y_at = lax.div(atoms_at, 32)
    near_base = dirs_at * HALF
    far_base = HALF - near_base

    def along(at, step, stride):
        return atoms_at + (lax.rem(at + step, 4) - at) * stride

    other_core = {"atoms": atoms_at + 1 - 2 * core}
    y_far = atoms_at + 32 - 64 * y_at
    y_peers = [
        {"atoms": y_far, "dirs": dirs_at},
        {"atoms": atoms_at, "dirs": 1 - dirs_at},
        {"atoms": y_far, "dirs": 1 - dirs_at},
    ]

    barrier = pltpu.get_barrier_semaphore()
    partners = [other_core] + y_peers
    for step in range(1, 4):
        partners += [{"atoms": along(x_at, step, 8)}, {"atoms": along(z_at, step, 2)}]
    for partner in partners:
        pl.semaphore_signal(
            barrier, inc=1, device_id=partner, device_id_type=pl.DeviceIdType.MESH
        )

    core_row = core * ROWS

    def place_of(g):
        odd = lax.rem(g, 2)
        first = x_at + odd * (z_at - x_at)
        second = z_at + odd * (x_at - z_at)
        return first, second, 8 - 6 * odd, 2 + 6 * odd

    def rows_of(g, step):
        first, _, _, _ = place_of(g)
        return core_row + lax.rem(first + step, 4) * FEAT

    def message(number, g):
        first, second, first_stride, second_stride = place_of(g)
        ahead = {"atoms": along(first, 1, first_stride)}
        behind = {"atoms": along(first, 3, first_stride)}
        first_row = core_row + first * FEAT
        second_row = first_row + second * 32
        y_row = second_row + y_at * 16
        if number == CORE_RS:
            src = part.at[g, tile_of((1 - core) * ROWS, ROWS, ROWS)]
            dst, to = core_in.at[g], other_core
        elif number < HOP_RS:
            side = number - RING_RS
            src = core_sum.at[g, tile_of(lax.rem(first + 2, 4) * FEAT + 64 * side, 64, 64)]
            dst, to = ring_in.at[g, side], (ahead, behind)[side]
        elif number < LINE_RS:
            side = number - HOP_RS
            src, dst, to = relay.at[g, side], hop_in.at[g, side], (ahead, behind)[side]
        elif number < Y_RS:
            step = number - LINE_RS + 1
            src = line_sum.at[g, tile_of(lax.rem(second + step, 4) * 32, 32, 32)]
            dst, to = line_in.at[g, 3 - step], {"atoms": along(second, step, second_stride)}
        elif number == Y_RS:
            src = y_sum.at[g, tile_of((1 - y_at) * 16, 16, 16)]
            dst, to = y_in.at[g], y_peers[0]
        elif number < LINE_AG:
            src = dst = state.at[dirs_at, g, tile_of(y_row, 16, 16)]
            to = y_peers[number - Y_AG]
        elif number < RING_AG:
            src = dst = state.at[:, g, tile_of(second_row, 32, 32)]
            to = {"atoms": along(second, number - LINE_AG + 1, second_stride)}
        elif number < HOP_AG:
            src = dst = state.at[:, g, tile_of(first_row, FEAT, FEAT)]
            to = (ahead, behind)[number - RING_AG]
        elif number < CORE_AG:
            side = number - HOP_AG
            src = dst = state.at[:, g, tile_of(rows_of(g, (3, 1)[side]) + 64 * side, 64, 64)]
            to = (ahead, behind)[side]
        else:
            src = dst = state.at[:, g, tile_of(core_row, ROWS, ROWS)]
            to = other_core
        return pltpu.make_async_remote_copy(
            src_ref=src,
            dst_ref=dst,
            send_sem=send_sem.at[number, g],
            recv_sem=recv_sem.at[number, g],
            device_id=to,
            device_id_type=pl.DeviceIdType.MESH,
        )

    first_of = (
        CORE_RS, RING_RS, HOP_RS, LINE_RS, Y_RS, Y_AG, LINE_AG, RING_AG, HOP_AG, CORE_AG, MESSAGES
    )

    def stage(number, g):
        if number > 0:
            for n in range(first_of[number - 1], first_of[number]):
                message(n, g).wait()
        if number == 1:
            mine = part[g, tile_of(core_row, ROWS, ROWS), :].astype(F32)
            core_sum[g] = (mine + core_in[g].astype(F32)).astype(BF16)
        elif number == 2:
            for side, step in ((0, 1), (1, 3)):
                rows = lax.rem(place_of(g)[0] + step, 4) * FEAT
                met, kept = rows + 64 * side, rows + 64 * (1 - side)
                total = core_sum[g, tile_of(met, 64, 64), :].astype(F32)
                total = total + ring_in[g, side].astype(F32)
                relay[g, side, 64 * side : 64 * side + 64, :] = total.astype(BF16)
                relay[g, side, 64 * (1 - side) : 64 * (1 - side) + 64, :] = core_sum[
                    g, tile_of(kept, 64, 64), :
                ]
        elif number == 3:
            total = core_sum[g, tile_of(place_of(g)[0] * FEAT, FEAT, FEAT), :].astype(F32)
            total = total + hop_in[g, 0].astype(F32) + hop_in[g, 1].astype(F32)
            line_sum[g] = total.astype(BF16)
        elif number == 4:
            total = line_sum[g, tile_of(place_of(g)[1] * 32, 32, 32), :].astype(F32)
            for slot in range(3):
                total = total + line_in[g, slot].astype(F32)
            y_sum[g] = total
        elif number == 5:
            first, second, _, _ = place_of(g)
            row = core_row + first * FEAT + second * 32 + y_at * 16
            total = y_sum[g, tile_of(y_at * 16, 16, 16), :] + y_in[g]
            state[dirs_at, g, tile_of(row, 16, 16), :] = total.astype(BF16)
        if number < STAGES - 1:
            for n in range(first_of[number], first_of[number + 1]):
                message(n, g).start()

    def exchange(t, lowest, highest):
        for number in range(STAGES - 1, -1, -1):
            if highest < number or lowest - number >= STEPS:
                continue
            if lowest >= number and highest - number < STEPS:
                stage(number, t - number)
            else:

                @pl.when(jnp.logical_and(t >= number, t < number + STEPS))
                def _(number=number):
                    stage(number, t - number)

    dirs_send[...] = jnp.zeros_like(dirs_send)
    dirs_send[0:3, 0:DIRS] = dirs_rows_ref[...]
    for f in range(FREQS):
        freq_tile[f : f + 1, :] = jnp.full((1, 128), freq_ref[f] * (0.5 / math.pi), F32)
    for base, low in ((near_base, 0), (far_base, HALF)):
        columns = tile_of(base, HALF, HALF)
        for axis in range(3):
            pos_tile[axis, :, low : low + HALF] = jnp.broadcast_to(
                pos_ref[axis : axis + 1, columns], (8, HALF)
            )
        alive_tile[:, low : low + HALF] = jnp.broadcast_to(
            jnp.where(domain_ref[:, columns] == atoms_at, 1.0, 0.0), (8, HALF)
        )
    for s in range(gain_ref.shape[0]):
        gain_tile[s] = jnp.broadcast_to(gain_ref[s : s + 1, :], (FEAT, FEAT)).T

    def alive_of(place):
        return jnp.concatenate([alive_tile[:, place]] * (FEAT // 8), axis=0)

    def gain_of(place, columns):
        species = jnp.broadcast_to(species_ref[:, columns], (FEAT, 128))
        gain = gain_tile[0]
        for s in range(1, gain_ref.shape[0]):
            gain = jnp.where(species == s, gain_tile[s], gain)
        return gain * alive_of(place)

    def prepare(block, carry):
        for base, low in ((near_base, 0), (far_base, HALF)):
            columns = tile_of(base + block * 128, 128, 128)
            place = tile_of(low + block * 128, 128, 128)
            keys = k_ref[columns, :].astype(F32).T * gain_of(place, columns)
            key_t[:, place] = keys.astype(BF16)
            query_t[:, place] = (q_ref[columns, :].astype(F32).T * alive_of(place)).astype(BF16)
            if low == 0:
                value_t[:, place] = v_ref[columns, :].astype(F32).T.astype(BF16)
                grad_t[:, place] = g_ref[columns, :].astype(F32).T.astype(BF16)
        return carry

    lax.fori_loop(0, HALF // 128, prepare, 0)

    def coef(u):
        return weight_ref[u] * mask_ref[u].astype(F32) * (1.0 / math.sqrt(FEAT * ATOMS))

    def rotate_to(x_ref, y_ref, u, p, columns, cosine, sine):
        lead = x_ref[p : p + 16, columns]
        trail = x_ref[p + 64 : p + 80, columns]
        y_ref[u, p : p + 16, columns] = lead * cosine - trail * sine
        y_ref[u, p + 64 : p + 80, columns] = lead * sine + trail * cosine

    def angles(dirs, at, columns):
        projected = (
            dirs[0, at] * pos_tile[0, :, columns]
            + dirs[1, at] * pos_tile[1, :, columns]
            + dirs[2, at] * pos_tile[2, :, columns]
        )
        for low_f in range(0, FREQS, 16):
            pairs = []
            for f in (low_f, low_f + 8):
                freq = jnp.concatenate([freq_tile[f : f + 8, :]] * (WIDTH // 128), axis=1)
                pairs.append(cos_sin_turns(projected * freq))
            cosine = jnp.concatenate([pairs[0][0], pairs[1][0]], axis=0).astype(BF16)
            sine = jnp.concatenate([pairs[0][1], pairs[1][1]], axis=0).astype(BF16)
            yield low_f, cosine, sine

    def state_step(i):
        for u in range(GROUP):
            at = i * GROUP + u
            for low in range(0, ATOMS, WIDTH):
                columns = pl.ds(low, WIDTH)
                for low_f, cosine, sine in angles(dirs_ref, at, columns):
                    if low < HALF:
                        cos_sin[at, 0, low_f : low_f + 16, columns] = cosine
                        cos_sin[at, 1, low_f : low_f + 16, columns] = sine
                    for p in (low_f, low_f + FREQS):
                        rotate_to(key_t, key_rot, u, p, columns, cosine, sine)
                        rotate_to(query_t, query_rot, u, p, columns, cosine, sine)
        for at_row, rotated, rows in ((0, key_rot, v_ref), (ROWS, query_rot, g_ref)):
            product = jnp.zeros((ROWS, FEAT), F32)
            for base, low in ((near_base, 0), (far_base, HALF)):
                product = product + jnp.dot(
                    rotated[:, :, low : low + HALF].reshape(ROWS, HALF),
                    rows[tile_of(base, HALF, HALF), :],
                    preferred_element_type=F32,
                )
            for u in range(GROUP):
                part[i, at_row + u * FEAT : at_row + (u + 1) * FEAT, :] = (
                    product[u * FEAT : (u + 1) * FEAT] * coef(i * GROUP + u)
                ).astype(BF16)

    def output_step(i, far):
        low_at = far * HALF
        for u in range(GROUP):
            at = i * GROUP + u
            for low in range(0, HALF, WIDTH):
                columns = pl.ds(low, WIDTH)
                if far:
                    table = angles(far_dirs, at, columns)
                else:
                    table = (
                        (
                            low_f,
                            cos_sin[at, 0, low_f : low_f + 16, columns],
                            cos_sin[at, 1, low_f : low_f + 16, columns],
                        )
                        for low_f in range(0, FREQS, 16)
                    )
                for low_f, cosine, sine in table:
                    if far:
                        far_cos_sin[u, 0, low_f : low_f + 16, columns] = cosine
                        far_cos_sin[u, 1, low_f : low_f + 16, columns] = sine
                    for p in (low_f, low_f + FREQS):
                        for x_ref, y_ref in ((key_t, key_rot), (query_t, query_rot)):
                            lead = x_ref[p : p + 16, columns]
                            trail = x_ref[p + 64 : p + 80, columns]
                            place = pl.ds(low_at + low, WIDTH)
                            y_ref[u, p : p + 16, place] = lead * cosine - trail * sine
                            y_ref[u, p + 64 : p + 80, place] = lead * sine + trail * cosine
        owner = 1 - dirs_at if far else dirs_at
        forward = state[owner, i, :ROWS, :]
        backward = state[owner, i, ROWS:, :]
        contract = (((0,), (0,)), ((), ()))
        for matrix, rotated, rows_t, total, back in (
            (forward, query_rot, grad_t, att_acc, back_q),
            (backward, key_rot, value_t, gv_acc, back_k),
        ):
            back[far] = (
                jnp.dot(matrix, rows_t[...], preferred_element_type=F32)
                .astype(BF16)
                .reshape(GROUP, FEAT, HALF)
            )
            total[...] += lax.dot_general(
                matrix,
                rotated[:, :, low_at : low_at + HALF].reshape(ROWS, HALF),
                contract,
                preferred_element_type=F32,
            )
        for low in range(0, HALF, WIDTH):
            columns = pl.ds(low, WIDTH)
            for low_f in range(0, FREQS, 16):
                if far:
                    tables = [far_cos_sin[u, :, low_f : low_f + 16, columns] for u in range(GROUP)]
                else:
                    tables = [
                        cos_sin[i * GROUP + u, :, low_f : low_f + 16, columns] for u in range(GROUP)
                    ]
                for p in (low_f, low_f + FREQS):
                    for back, total in ((back_q, gq_acc), (back_k, gk_acc)):
                        lead_sum = trail_sum = None
                        for u in range(GROUP):
                            cosine, sine = tables[u][0], tables[u][1]
                            lead = back[far, u, p : p + 16, columns]
                            trail = back[far, u, p + 64 : p + 80, columns]
                            new_lead = lead * cosine + trail * sine
                            new_trail = trail * cosine - lead * sine
                            lead_sum = new_lead if u == 0 else lead_sum + new_lead
                            trail_sum = new_trail if u == 0 else trail_sum + new_trail
                        total[p : p + 16, columns] += lead_sum.astype(F32)
                        total[p + 64 : p + 80, columns] += trail_sum.astype(F32)

    totals = (att_acc, gq_acc, gk_acc, gv_acc)
    for total in totals:
        total[...] = jnp.zeros_like(total)

    pl.semaphore_wait(barrier, len(partners))

    dirs_copy = pltpu.make_async_remote_copy(
        src_ref=dirs_send,
        dst_ref=dirs_recv,
        send_sem=dirs_sem.at[0],
        recv_sem=dirs_sem.at[1],
        device_id=y_peers[1],
        device_id_type=pl.DeviceIdType.MESH,
    )
    dirs_copy.start()

    def first_loop(t, carry):
        state_step(t)
        exchange(t, 0, STEPS - 1)
        return carry

    lax.fori_loop(0, STEPS, first_loop, 0)

    dirs_copy.wait()
    to_scalars = pltpu.make_async_copy(dirs_recv, far_dirs, dirs_sem.at[2])
    to_scalars.start()
    to_scalars.wait()

    def second_loop(i, carry):
        exchange(i + STEPS, STEPS, 2 * STEPS - 1)
        output_step(i, 0)
        output_step(i, 1)
        return carry

    lax.fori_loop(0, STEPS, second_loop, 0)

    def finish(block, carry):
        place = tile_of(block * 128, 128, 128)
        alive = alive_of(place)
        gain = gain_of(place, tile_of(near_base + block * 128, 128, 128))
        for total, out, factor in zip(
            totals, (att_out, gq_out, gk_out, gv_out), (None, alive, gain, None)
        ):
            whole = total[:, place]
            if factor is not None:
                whole = whole * factor
            out[place, :] = whole.T.astype(BF16)
        return carry

    lax.fori_loop(0, HALF // 128, finish, 0)


def per_device(
    queries,
    keys,
    values,
    cotangent,
    positions,
    species,
    domain,
    species_gain,
    frequency,
    directions,
    dir_weight,
    dir_mask,
):
    smem = pl.BlockSpec(memory_space=pltpu.SMEM)
    vmem = pl.BlockSpec(memory_space=pltpu.VMEM)
    species_count = species_gain.shape[0]
    scratch = [
        pltpu.VMEM((FREQS, 128), F32),
        pltpu.VMEM((3, 8, ATOMS), F32),
        pltpu.VMEM((species_count, FEAT, FEAT), F32),
        pltpu.VMEM((8, ATOMS), F32),
        pltpu.VMEM((FEAT, ATOMS), BF16),
        pltpu.VMEM((FEAT, ATOMS), BF16),
        pltpu.VMEM((FEAT, HALF), BF16),
        pltpu.VMEM((FEAT, HALF), BF16),
        pltpu.VMEM((DIRS, 2, FREQS, HALF), BF16),
        pltpu.VMEM((GROUP, 2, FREQS, HALF), BF16),
        pltpu.VMEM((GROUP, FEAT, ATOMS), BF16),
        pltpu.VMEM((GROUP, FEAT, ATOMS), BF16),
        pltpu.VMEM((2, GROUP, FEAT, HALF), BF16),
        pltpu.VMEM((2, GROUP, FEAT, HALF), BF16),
        pltpu.VMEM((FEAT, HALF), F32),
        pltpu.VMEM((FEAT, HALF), F32),
        pltpu.VMEM((FEAT, HALF), F32),
        pltpu.VMEM((FEAT, HALF), F32),
        pltpu.VMEM((STEPS, 2 * ROWS, FEAT), BF16),
        pltpu.VMEM((STEPS, ROWS, FEAT), BF16),
        pltpu.VMEM((STEPS, ROWS, FEAT), BF16),
        pltpu.VMEM((STEPS, 2, 64, FEAT), BF16),
        pltpu.VMEM((STEPS, 2, FEAT, FEAT), BF16),
        pltpu.VMEM((STEPS, 2, FEAT, FEAT), BF16),
        pltpu.VMEM((STEPS, FEAT, FEAT), BF16),
        pltpu.VMEM((STEPS, 3, 32, FEAT), BF16),
        pltpu.VMEM((STEPS, 32, FEAT), F32),
        pltpu.VMEM((STEPS, 16, FEAT), F32),
        pltpu.VMEM((2, STEPS, 2 * ROWS, FEAT), BF16),
        pltpu.VMEM((8, 128), F32),
        pltpu.VMEM((8, 128), F32),
        pltpu.SMEM((8, 128), F32),
        pltpu.SemaphoreType.DMA((MESSAGES, STEPS)),
        pltpu.SemaphoreType.DMA((MESSAGES, STEPS)),
        pltpu.SemaphoreType.DMA((3,)),
    ]
    att, gq, gk, gv = pl.pallas_call(
        kernel,
        out_shape=[jax.ShapeDtypeStruct((HALF, FEAT), BF16)] * 4,
        in_specs=[smem] * 4 + [vmem] * 9,
        out_specs=[vmem] * 4,
        scratch_shapes=scratch,
        compiler_params=pltpu.CompilerParams(
            collective_id=0, has_side_effects=True, vmem_limit_bytes=56 * 2**20
        ),
        name="fast_attention",
    )(
        frequency,
        directions,
        dir_weight,
        dir_mask,
        directions,
        queries,
        keys,
        values,
        cotangent,
        positions,
        species.reshape(1, ATOMS),
        domain.reshape(1, ATOMS),
        species_gain,
    )
    return att, gq, gk, gv


def solution(mesh):
    return jax.shard_map(
        per_device,
        mesh=mesh,
        in_specs=(
            P("atoms", None),
            P("atoms", None),
            P("atoms", None),
            P("atoms", None),
            P(None, "atoms"),
            P("atoms"),
            P("atoms"),
            P(),
            P(),
            P(None, "dirs"),
            P("dirs"),
            P("dirs"),
        ),
        out_specs=(
            P(("atoms", "dirs"), None),
            P(("atoms", "dirs"), None),
            P(("atoms", "dirs"), None),
            P(("atoms", "dirs"), None),
        ),
        check_vma=False,
    )
```

```python
import itertools
import math

import jax
import jax.numpy as jnp
from jax import lax
from jax.experimental import pallas as pl
from jax.experimental.pallas import tpu as pltpu
from jax.sharding import PartitionSpec as P

F32 = jnp.float32
BF16 = jnp.bfloat16

ATOMS = 2048
HALF = ATOMS // 2
FEAT = 128
FREQS = 32
DIRS = 44
GROUP = 4
STEPS = DIRS // GROUP
ROWS = GROUP * FEAT
WIDTH = 256

SINE = (
    4.442882919124345,
    -7.3082456865090855,
    3.606354218433185,
    -0.8461116503751638,
    0.10982451642692614,
)
COSINE = (
    1.4142134962552289,
    -6.978850948563847,
    5.739460376907657,
    -1.8835579059891776,
    0.3106880275307806,
)

ORDERS = (('x', 'y', 'z'), ('z', 'y', 'x'))
SIZE = {"c": 2, "x": 4, "z": 4, "y": 2}
STAGES = 9
FILL = 4
TICKS = (
    (),
    ((0, 0),),
    (),
    ((0, 1), (1, 0)),
    (),
    ((1, 1), (2, 0)),
    (),
    ((2, 1), (3, 0)),
    ((0, 2),),
    ((3, 1), (4, 0)),
    ((1, 2),),
    ((4, 1), (5, 0)),
    ((0, 3), (2, 2)),
    ((5, 1), (6, 0)),
    ((1, 3), (3, 2)),
    ((6, 1), (7, 0)),
    ((0, 4), (2, 3), (4, 2)),
    ((7, 1), (8, 0)),
    ((1, 4), (3, 3), (5, 2)),
    ((8, 1), (9, 0)),
    ((0, 5), (2, 4), (4, 3), (6, 2)),
    ((9, 1), (10, 0)),
    (),
    ((1, 5), (3, 4), (5, 3), (7, 2)),
    ((10, 1),),
    ((0, 6), (2, 5), (4, 4), (6, 3), (8, 2)),
    ((3, 5), (5, 4), (1, 6), (9, 2), (7, 3), (4, 5), (10, 2), (6, 4), (2, 6), (8, 3), (3, 6), (9, 3), (0, 7), (5, 5), (7, 4), (4, 6), (1, 7), (10, 3), (6, 5), (8, 4), (0, 8)),
    (),
    ((1, 8), (2, 7), (5, 6), (7, 5), (9, 4)),
    ((3, 7), (6, 6), (8, 5), (10, 4)),
    ((2, 8), (4, 7)),
    ((3, 8), (9, 5)),
    ((7, 6),),
    ((4, 8), (5, 7), (8, 6), (10, 5)),
    ((6, 7),),
    ((5, 8), (9, 6)),
    (),
    ((6, 8), (10, 6)),
    ((7, 7),),
    ((8, 7),),
    ((7, 8),),
    ((9, 7),),
    ((8, 8),),
    ((10, 7),),
    ((9, 8),),
    (),
    ((10, 8),),
    (),
)


def levels_of(g):
    levels, rows, taken, kept = [], 2 * ROWS, 0, 0
    for axes in ("c",) + ORDERS[g % len(ORDERS)]:
        count = math.prod(SIZE[axis] for axis in axes)
        rows //= count
        levels.append((axes, rows, taken, kept))
        taken += (count - 1) * rows
        kept += rows
    return levels


def offsets_of(axes, gather):
    choices = []
    for axis in axes:
        if gather and axis == "y":
            choices.append([{"y": h, "d": d} for h in range(2) for d in range(2)])
        else:
            choices.append([{axis: step} for step in range(SIZE[axis])])
    merged = [{k: v for part in parts for k, v in part.items()} for parts in itertools.product(*choices)]
    return [steps for steps in merged if any(steps.values())]


def first_messages(g):
    levels = levels_of(g)
    counts = [len(offsets_of(axes, False)) for axes, _, _, _ in levels]
    counts += [len(offsets_of(axes, True)) for axes, _, _, _ in levels[::-1]]
    return [sum(counts[:n]) for n in range(len(counts) + 1)]


MESSAGES = max(first_messages(g)[-1] for g in range(STEPS))


def horner(coefficients, square):
    total = square * coefficients[-1] + coefficients[-2]
    for coefficient in coefficients[-3::-1]:
        total = total * square + coefficient
    return total


def cos_sin_turns(turns):
    nearest = (turns + 12582912.0) - 12582912.0
    rest = turns - nearest
    square = rest * rest
    sine = horner(SINE, square) * rest
    cosine = horner(COSINE, square)
    return 1.0 - sine * sine, sine * cosine


def tile_of(start, size, unit):
    return pl.ds(pl.multiple_of(start, unit), size)


def kernel(
    freq_ref,
    dirs_ref,
    weight_ref,
    mask_ref,
    dirs_rows_ref,
    q_ref,
    k_ref,
    v_ref,
    g_ref,
    pos_ref,
    species_ref,
    domain_ref,
    gain_ref,
    att_out,
    gq_out,
    gk_out,
    gv_out,
    freq_tile,
    pos_tile,
    gain_tile,
    alive_tile,
    key_t,
    query_t,
    value_t,
    grad_t,
    cos_sin,
    key_rot,
    query_rot,
    back_q,
    back_k,
    att_acc,
    gv_acc,
    gq_acc,
    gk_acc,
    part,
    taken_in,
    kept_sum,
    state,
    dirs_send,
    dirs_recv,
    far_dirs,
    send_sem,
    recv_sem,
    dirs_sem,
):
    atoms_at = lax.axis_index("atoms")
    dirs_at = lax.axis_index("dirs")
    core = lax.rem(atoms_at, 2)
    z_at = lax.rem(lax.div(atoms_at, 2), 4)
    x_at = lax.rem(lax.div(atoms_at, 8), 4)
    y_at = lax.div(atoms_at, 32)
    near_base = dirs_at * HALF
    far_base = HALF - near_base

    place = {"c": core, "x": x_at, "z": z_at, "y": y_at}

    def device(steps):
        at = {axis: lax.rem(place[axis] + steps.get(axis, 0), SIZE[axis]) for axis in place}
        to = {"atoms": ((at["y"] * 4 + at["x"]) * 4 + at["z"]) * 2 + at["c"]}
        if steps.get("d", 0):
            to["dirs"] = 1 - dirs_at
        return to

    def part_of(axes, steps):
        index = 0
        for axis in axes:
            index = index * SIZE[axis] + lax.rem(place[axis] + steps.get(axis, 0), SIZE[axis])
        return index

    met = []
    for g in range(STEPS):
        for axes, _, _, _ in levels_of(g):
            met += [steps for steps in offsets_of(axes, True) if steps not in met]
    met += [steps for steps in ({"d": 1},) if {"y": 0, "d": 1} not in met]
    barrier = pltpu.get_barrier_semaphore()
    partners = [device(steps) for steps in met]
    for partner in partners:
        pl.semaphore_signal(
            barrier, inc=1, device_id=partner, device_id_type=pl.DeviceIdType.MESH
        )

    def state_rows(g, level):
        start = 0
        for axes, rows, _, _ in levels_of(g)[: level + 1]:
            start = start + part_of(axes, {}) * rows
        rows = levels_of(g)[level][1]
        return tile_of(start, rows, rows)

    def messages(number, g):
        levels = levels_of(g)
        first = first_messages(g)[number]
        result = []
        if number < len(levels):
            axes, rows, taken, _ = levels[number]
            for n, steps in enumerate(offsets_of(axes, False)):
                start = part_of(axes, steps) * rows
                if number == 0:
                    src = part.at[g, tile_of(start, rows, rows)]
                else:
                    src = kept_sum.at[g, tile_of(levels[number - 1][3] + start, rows, rows)]
                dst = taken_in.at[g, taken + n * rows : taken + (n + 1) * rows]
                result.append((src, dst, steps))
        else:
            level = 2 * len(levels) - 1 - number
            whole = any("y" in axes for axes, _, _, _ in levels[level + 1 :])
            here = state.at[slice(None) if whole else dirs_at, g, state_rows(g, level)]
            result = [(here, here, steps) for steps in offsets_of(levels[level][0], True)]
        return [
            pltpu.make_async_remote_copy(
                src_ref=src,
                dst_ref=dst,
                send_sem=send_sem.at[g, first + n],
                recv_sem=recv_sem.at[g, first + n],
                device_id=device(steps),
                device_id_type=pl.DeviceIdType.MESH,
            )
            for n, (src, dst, steps) in enumerate(result)
        ]

    def stage(number, g):
        levels = levels_of(g)
        depth = len(levels)
        if number > 0:
            for copy in messages(number - 1, g):
                copy.wait()
        if 0 < number <= depth:
            axes, rows, taken, kept = levels[number - 1]
            start = part_of(axes, {}) * rows
            if number == 1:
                total = part[g, tile_of(start, rows, rows), :].astype(F32)
            else:
                total = kept_sum[g, tile_of(levels[number - 2][3] + start, rows, rows), :].astype(F32)
            for n in range(math.prod(SIZE[axis] for axis in axes) - 1):
                total = total + taken_in[g, taken + n * rows : taken + (n + 1) * rows, :].astype(F32)
            if number == depth:
                state[dirs_at, g, state_rows(g, depth - 1), :] = total.astype(BF16)
            else:
                kept_sum[g, kept : kept + rows, :] = total.astype(BF16)
        if number < 2 * depth:
            for copy in messages(number, g):
                copy.start()

    def exchange(t, ticks):
        for tick in ticks:
            if TICKS[tick]:

                @pl.when(t == tick)
                def _(tick=tick):
                    for g, number in TICKS[tick]:
                        stage(number, g)

    dirs_send[...] = jnp.zeros_like(dirs_send)
    dirs_send[0:3, 0:DIRS] = dirs_rows_ref[...]
    for f in range(FREQS):
        freq_tile[f : f + 1, :] = jnp.full((1, 128), freq_ref[f] * (0.5 / math.pi), F32)
    for base, low in ((near_base, 0), (far_base, HALF)):
        columns = tile_of(base, HALF, HALF)
        for axis in range(3):
            pos_tile[axis, :, low : low + HALF] = jnp.broadcast_to(
                pos_ref[axis : axis + 1, columns], (8, HALF)
            )
        alive_tile[:, low : low + HALF] = jnp.broadcast_to(
            jnp.where(domain_ref[:, columns] == atoms_at, 1.0, 0.0), (8, HALF)
        )
    for s in range(gain_ref.shape[0]):
        gain_tile[s] = jnp.broadcast_to(gain_ref[s : s + 1, :], (FEAT, FEAT)).T

    def alive_of(place):
        return jnp.concatenate([alive_tile[:, place]] * (FEAT // 8), axis=0)

    def gain_of(place, columns):
        species = jnp.broadcast_to(species_ref[:, columns], (FEAT, 128))
        gain = gain_tile[0]
        for s in range(1, gain_ref.shape[0]):
            gain = jnp.where(species == s, gain_tile[s], gain)
        return gain * alive_of(place)

    def prepare(block, carry):
        for base, low in ((near_base, 0), (far_base, HALF)):
            columns = tile_of(base + block * 128, 128, 128)
            place = tile_of(low + block * 128, 128, 128)
            keys = k_ref[columns, :].astype(F32).T * gain_of(place, columns)
            key_t[:, place] = keys.astype(BF16)
            query_t[:, place] = (q_ref[columns, :].astype(F32).T * alive_of(place)).astype(BF16)
            if low == 0:
                value_t[:, place] = v_ref[columns, :].astype(F32).T.astype(BF16)
                grad_t[:, place] = g_ref[columns, :].astype(F32).T.astype(BF16)
        return carry

    lax.fori_loop(0, HALF // 128, prepare, 0)

    def coef(u):
        return weight_ref[u] * mask_ref[u].astype(F32) * (1.0 / math.sqrt(FEAT * ATOMS))

    def rotate_to(x_ref, y_ref, u, p, columns, cosine, sine):
        lead = x_ref[p : p + 16, columns]
        trail = x_ref[p + 64 : p + 80, columns]
        y_ref[u, p : p + 16, columns] = lead * cosine - trail * sine
        y_ref[u, p + 64 : p + 80, columns] = lead * sine + trail * cosine

    def angles(dirs, at, columns):
        projected = (
            dirs[0, at] * pos_tile[0, :, columns]
            + dirs[1, at] * pos_tile[1, :, columns]
            + dirs[2, at] * pos_tile[2, :, columns]
        )
        for low_f in range(0, FREQS, 16):
            pairs = []
            for f in (low_f, low_f + 8):
                freq = jnp.concatenate([freq_tile[f : f + 8, :]] * (WIDTH // 128), axis=1)
                pairs.append(cos_sin_turns(projected * freq))
            cosine = jnp.concatenate([pairs[0][0], pairs[1][0]], axis=0).astype(BF16)
            sine = jnp.concatenate([pairs[0][1], pairs[1][1]], axis=0).astype(BF16)
            yield low_f, cosine, sine

    def state_step(i):
        for u in range(GROUP):
            if u == GROUP // 2:
                exchange(2 * i, range(0, 2 * STEPS, 2))
            at = i * GROUP + u
            for low in range(0, ATOMS, WIDTH):
                columns = pl.ds(low, WIDTH)
                for low_f, cosine, sine in angles(dirs_ref, at, columns):
                    if low < HALF:
                        cos_sin[at, 0, low_f : low_f + 16, columns] = cosine
                        cos_sin[at, 1, low_f : low_f + 16, columns] = sine
                    for p in (low_f, low_f + FREQS):
                        rotate_to(key_t, key_rot, u, p, columns, cosine, sine)
                        rotate_to(query_t, query_rot, u, p, columns, cosine, sine)
        for at_row, rotated, rows in ((0, key_rot, v_ref), (ROWS, query_rot, g_ref)):
            product = jnp.zeros((ROWS, FEAT), F32)
            for base, low in ((near_base, 0), (far_base, HALF)):
                product = product + jnp.dot(
                    rotated[:, :, low : low + HALF].reshape(ROWS, HALF),
                    rows[tile_of(base, HALF, HALF), :],
                    preferred_element_type=F32,
                )
            for u in range(GROUP):
                part[i, at_row + u * FEAT : at_row + (u + 1) * FEAT, :] = (
                    product[u * FEAT : (u + 1) * FEAT] * coef(i * GROUP + u)
                ).astype(BF16)

    def far_angles(at):
        for low in range(0, HALF, WIDTH):
            columns = pl.ds(low, WIDTH)
            for low_f, cosine, sine in angles(far_dirs, at, columns):
                cos_sin[DIRS + at, 0, low_f : low_f + 16, columns] = cosine
                cos_sin[DIRS + at, 1, low_f : low_f + 16, columns] = sine

    def output_step(i, far):
        low_at = far * HALF
        table_at = far * DIRS + i * GROUP
        for u in range(GROUP):
            for low in range(0, HALF, WIDTH):
                columns = pl.ds(low, WIDTH)
                place = pl.ds(low_at + low, WIDTH)
                for low_f in range(0, FREQS, 16):
                    cosine = cos_sin[table_at + u, 0, low_f : low_f + 16, columns]
                    sine = cos_sin[table_at + u, 1, low_f : low_f + 16, columns]
                    for p in (low_f, low_f + FREQS):
                        for x_ref, y_ref in ((key_t, key_rot), (query_t, query_rot)):
                            lead = x_ref[p : p + 16, columns]
                            trail = x_ref[p + 64 : p + 80, columns]
                            y_ref[u, p : p + 16, place] = lead * cosine - trail * sine
                            y_ref[u, p + 64 : p + 80, place] = lead * sine + trail * cosine
        owner = 1 - dirs_at if far else dirs_at
        forward = state[owner, i, :ROWS, :]
        backward = state[owner, i, ROWS:, :]
        contract = (((0,), (0,)), ((), ()))
        for matrix, rotated, rows_t, total, back in (
            (forward, query_rot, grad_t, att_acc, back_q),
            (backward, key_rot, value_t, gv_acc, back_k),
        ):
            back[far] = (
                jnp.dot(matrix, rows_t[...], preferred_element_type=F32)
                .astype(BF16)
                .reshape(GROUP, FEAT, HALF)
            )
            total[...] += lax.dot_general(
                matrix,
                rotated[:, :, low_at : low_at + HALF].reshape(ROWS, HALF),
                contract,
                preferred_element_type=F32,
            )
        for low in range(0, HALF, WIDTH):
            columns = pl.ds(low, WIDTH)
            for low_f in range(0, FREQS, 16):
                tables = [
                    cos_sin[table_at + u, :, low_f : low_f + 16, columns] for u in range(GROUP)
                ]
                for p in (low_f, low_f + FREQS):
                    for back, total in ((back_q, gq_acc), (back_k, gk_acc)):
                        lead_sum = trail_sum = None
                        for u in range(GROUP):
                            cosine, sine = tables[u][0], tables[u][1]
                            lead = back[far, u, p : p + 16, columns]
                            trail = back[far, u, p + 64 : p + 80, columns]
                            new_lead = lead * cosine + trail * sine
                            new_trail = trail * cosine - lead * sine
                            lead_sum = new_lead if u == 0 else lead_sum + new_lead
                            trail_sum = new_trail if u == 0 else trail_sum + new_trail
                        total[p : p + 16, columns] += lead_sum.astype(F32)
                        total[p + 64 : p + 80, columns] += trail_sum.astype(F32)

    totals = (att_acc, gq_acc, gk_acc, gv_acc)
    for total in totals:
        total[...] = jnp.zeros_like(total)

    pl.semaphore_wait(barrier, len(partners))

    dirs_copy = pltpu.make_async_remote_copy(
        src_ref=dirs_send,
        dst_ref=dirs_recv,
        send_sem=dirs_sem.at[0],
        recv_sem=dirs_sem.at[1],
        device_id={"dirs": 1 - dirs_at},
        device_id_type=pl.DeviceIdType.MESH,
    )
    dirs_copy.start()

    def first_loop(i, carry):
        state_step(i)
        exchange(2 * i + 1, range(1, 2 * STEPS, 2))
        return carry

    lax.fori_loop(0, STEPS, first_loop, 0)

    dirs_copy.wait()
    to_scalars = pltpu.make_async_copy(dirs_recv, far_dirs, dirs_sem.at[2])
    to_scalars.start()
    to_scalars.wait()

    def fill_loop(t, carry):
        exchange(t + 2 * STEPS, range(2 * STEPS, 2 * STEPS + FILL))

        def fill(n, inner):
            far_angles(t * (DIRS // FILL) + n)
            return inner

        return lax.fori_loop(0, DIRS // FILL, fill, carry)

    lax.fori_loop(0, FILL, fill_loop, 0)

    def second_loop(i, carry):
        at = 2 * STEPS + FILL
        for far in range(2):
            exchange(at + 2 * i + far, range(at + far, at + 2 * STEPS, 2))
            output_step(i, far)
        return carry

    lax.fori_loop(0, STEPS, second_loop, 0)

    def finish(block, carry):
        place = tile_of(block * 128, 128, 128)
        alive = alive_of(place)
        gain = gain_of(place, tile_of(near_base + block * 128, 128, 128))
        for total, out, factor in zip(
            totals, (att_out, gq_out, gk_out, gv_out), (None, alive, gain, None)
        ):
            whole = total[:, place]
            if factor is not None:
                whole = whole * factor
            out[place, :] = whole.T.astype(BF16)
        return carry

    lax.fori_loop(0, HALF // 128, finish, 0)


def per_device(
    queries,
    keys,
    values,
    cotangent,
    positions,
    species,
    domain,
    species_gain,
    frequency,
    directions,
    dir_weight,
    dir_mask,
):
    smem = pl.BlockSpec(memory_space=pltpu.SMEM)
    vmem = pl.BlockSpec(memory_space=pltpu.VMEM)
    species_count = species_gain.shape[0]
    scratch = [
        pltpu.VMEM((FREQS, 128), F32),
        pltpu.VMEM((3, 8, ATOMS), F32),
        pltpu.VMEM((species_count, FEAT, FEAT), F32),
        pltpu.VMEM((8, ATOMS), F32),
        pltpu.VMEM((FEAT, ATOMS), BF16),
        pltpu.VMEM((FEAT, ATOMS), BF16),
        pltpu.VMEM((FEAT, HALF), BF16),
        pltpu.VMEM((FEAT, HALF), BF16),
        pltpu.VMEM((2 * DIRS, 2, FREQS, HALF), BF16),
        pltpu.VMEM((GROUP, FEAT, ATOMS), BF16),
        pltpu.VMEM((GROUP, FEAT, ATOMS), BF16),
        pltpu.VMEM((2, GROUP, FEAT, HALF), BF16),
        pltpu.VMEM((2, GROUP, FEAT, HALF), BF16),
        pltpu.VMEM((FEAT, HALF), F32),
        pltpu.VMEM((FEAT, HALF), F32),
        pltpu.VMEM((FEAT, HALF), F32),
        pltpu.VMEM((FEAT, HALF), F32),
        pltpu.VMEM((STEPS, 2 * ROWS, FEAT), BF16),
        pltpu.VMEM((STEPS, 2 * ROWS, FEAT), BF16),
        pltpu.VMEM((STEPS, 2 * ROWS, FEAT), BF16),
        pltpu.VMEM((2, STEPS, 2 * ROWS, FEAT), BF16),
        pltpu.VMEM((8, 128), F32),
        pltpu.VMEM((8, 128), F32),
        pltpu.SMEM((8, 128), F32),
        pltpu.SemaphoreType.DMA((STEPS, MESSAGES)),
        pltpu.SemaphoreType.DMA((STEPS, MESSAGES)),
        pltpu.SemaphoreType.DMA((3,)),
    ]
    att, gq, gk, gv = pl.pallas_call(
        kernel,
        out_shape=[jax.ShapeDtypeStruct((HALF, FEAT), BF16)] * 4,
        in_specs=[smem] * 4 + [vmem] * 9,
        out_specs=[vmem] * 4,
        scratch_shapes=scratch,
        compiler_params=pltpu.CompilerParams(
            collective_id=0, has_side_effects=True, vmem_limit_bytes=56 * 2**20
        ),
        name="fast_attention",
    )(
        frequency,
        directions,
        dir_weight,
        dir_mask,
        directions,
        queries,
        keys,
        values,
        cotangent,
        positions,
        species.reshape(1, ATOMS),
        domain.reshape(1, ATOMS),
        species_gain,
    )
    return att, gq, gk, gv


def solution(mesh):
    return jax.shard_map(
        per_device,
        mesh=mesh,
        in_specs=(
            P("atoms", None),
            P("atoms", None),
            P("atoms", None),
            P("atoms", None),
            P(None, "atoms"),
            P("atoms"),
            P("atoms"),
            P(),
            P(),
            P(None, "dirs"),
            P("dirs"),
            P("dirs"),
        ),
        out_specs=(
            P(("atoms", "dirs"), None),
            P(("atoms", "dirs"), None),
            P(("atoms", "dirs"), None),
            P(("atoms", "dirs"), None),
        ),
        check_vma=False,
    )
```

```python
import itertools
import math

import jax
import jax.numpy as jnp
from jax import lax
from jax.experimental import pallas as pl
from jax.experimental.pallas import tpu as pltpu
from jax.sharding import PartitionSpec as P

F32 = jnp.float32
BF16 = jnp.bfloat16

ATOMS = 2048
HALF = ATOMS // 2
FEAT = 128
FREQS = 32
DIRS = 44
GROUP = 4
STEPS = DIRS // GROUP
ROWS = GROUP * FEAT
WIDTH = 256

SINE = (4.4428795675460835, -7.307816684491783, 3.59777417808721, -0.791199392161295)
COSINE = (1.4142040148090755, -6.977637323456294, 5.715187874756719, -1.7282138922235275)

ORDERS = (('x', 'y', 'z'), ('z', 'y', 'x'))
SIZE = {"c": 2, "x": 4, "z": 4, "y": 2}
STAGES = 9
FILL = 4
TICKS = (
    (),
    ((0, 0),),
    (),
    ((0, 1), (1, 0)),
    (),
    ((1, 1), (2, 0)),
    (),
    ((2, 1), (3, 0)),
    ((0, 2),),
    ((3, 1), (4, 0)),
    ((1, 2),),
    ((4, 1), (5, 0)),
    ((0, 3), (2, 2)),
    ((5, 1), (6, 0)),
    ((1, 3), (3, 2)),
    ((6, 1), (7, 0)),
    ((0, 4), (2, 3), (4, 2)),
    ((7, 1), (8, 0)),
    ((1, 4), (3, 3), (5, 2)),
    ((0, 5), (6, 2), (8, 1), (9, 0)),
    ((2, 4), (4, 3)),
    ((1, 5), (3, 4), (7, 2), (9, 1), (10, 0)),
    ((5, 3),),
    ((0, 6), (6, 3), (10, 1)),
    ((2, 5), (3, 5), (4, 4), (8, 2)),
    ((1, 6), (5, 4), (7, 3), (9, 2)),
    ((6, 4), (4, 5), (2, 6), (0, 7), (3, 6), (8, 3), (9, 3), (10, 2), (5, 5), (7, 4), (0, 8)),
    ((1, 7), (4, 6), (6, 5)),
    ((10, 3), (2, 7), (9, 4), (1, 8)),
    ((3, 7), (5, 6), (7, 5), (8, 4)),
    ((2, 8), (6, 6), (10, 4)),
    ((3, 8), (4, 7), (9, 5)),
    ((7, 6),),
    ((4, 8), (5, 7), (8, 5), (10, 5)),
    ((6, 7), (9, 6)),
    ((5, 8),),
    ((6, 8), (7, 7), (8, 6), (10, 6)),
    (),
    ((7, 8),),
    ((9, 7),),
    (),
    ((8, 7), (9, 8)),
    ((10, 7), (8, 8)),
    (),
    ((10, 8),),
    (),
    (),
    (),
)


def levels_of(g):
    levels, rows, taken, kept = [], 2 * ROWS, 0, 0
    for axes in ("c",) + ORDERS[g % len(ORDERS)]:
        count = math.prod(SIZE[axis] for axis in axes)
        rows //= count
        levels.append((axes, rows, taken, kept))
        taken += (count - 1) * rows
        kept += rows
    return levels


def offsets_of(axes, gather):
    choices = []
    for axis in axes:
        if gather and axis == "y":
            choices.append([{"y": h, "d": d} for h in range(2) for d in range(2)])
        else:
            choices.append([{axis: step} for step in range(SIZE[axis])])
    merged = [{k: v for part in parts for k, v in part.items()} for parts in itertools.product(*choices)]
    return [steps for steps in merged if any(steps.values())]


def first_messages(g):
    levels = levels_of(g)
    counts = [len(offsets_of(axes, False)) for axes, _, _, _ in levels]
    counts += [len(offsets_of(axes, True)) for axes, _, _, _ in levels[::-1]]
    return [sum(counts[:n]) for n in range(len(counts) + 1)]


MESSAGES = max(first_messages(g)[-1] for g in range(STEPS))


def horner(coefficients, square):
    total = square * coefficients[-1] + coefficients[-2]
    for coefficient in coefficients[-3::-1]:
        total = total * square + coefficient
    return total


def cos_sin_turns(turns):
    rest = turns - jnp.round(turns)
    square = rest * rest
    sine = horner(SINE, square) * rest
    cosine = horner(COSINE, square)
    return 1.0 - sine * sine, sine * cosine


def tile_of(start, size, unit):
    return pl.ds(pl.multiple_of(start, unit), size)


def kernel(
    freq_ref,
    dirs_ref,
    weight_ref,
    mask_ref,
    dirs_rows_ref,
    q_ref,
    k_ref,
    v_ref,
    g_ref,
    pos_ref,
    species_ref,
    domain_ref,
    gain_ref,
    att_out,
    gq_out,
    gk_out,
    gv_out,
    freq_tile,
    pos_tile,
    gain_tile,
    alive_tile,
    key_t,
    query_t,
    value_t,
    grad_t,
    cos_sin,
    key_rot,
    query_rot,
    back_q,
    back_k,
    att_acc,
    gv_acc,
    gq_acc,
    gk_acc,
    part,
    taken_in,
    kept_sum,
    state,
    dirs_send,
    dirs_recv,
    far_dirs,
    send_sem,
    recv_sem,
    dirs_sem,
):
    atoms_at = lax.axis_index("atoms")
    dirs_at = lax.axis_index("dirs")
    core = lax.rem(atoms_at, 2)
    z_at = lax.rem(lax.div(atoms_at, 2), 4)
    x_at = lax.rem(lax.div(atoms_at, 8), 4)
    y_at = lax.div(atoms_at, 32)
    near_base = dirs_at * HALF
    far_base = HALF - near_base

    place = {"c": core, "x": x_at, "z": z_at, "y": y_at}

    def device(steps):
        at = {axis: lax.rem(place[axis] + steps.get(axis, 0), SIZE[axis]) for axis in place}
        to = {"atoms": ((at["y"] * 4 + at["x"]) * 4 + at["z"]) * 2 + at["c"]}
        if steps.get("d", 0):
            to["dirs"] = 1 - dirs_at
        return to

    def part_of(axes, steps):
        index = 0
        for axis in axes:
            index = index * SIZE[axis] + lax.rem(place[axis] + steps.get(axis, 0), SIZE[axis])
        return index

    met = []
    for g in range(STEPS):
        for axes, _, _, _ in levels_of(g):
            met += [steps for steps in offsets_of(axes, True) if steps not in met]
    met += [steps for steps in ({"d": 1},) if {"y": 0, "d": 1} not in met]
    barrier = pltpu.get_barrier_semaphore()
    partners = [device(steps) for steps in met]
    for partner in partners:
        pl.semaphore_signal(
            barrier, inc=1, device_id=partner, device_id_type=pl.DeviceIdType.MESH
        )

    def state_rows(g, level):
        start = 0
        for axes, rows, _, _ in levels_of(g)[: level + 1]:
            start = start + part_of(axes, {}) * rows
        rows = levels_of(g)[level][1]
        return tile_of(start, rows, rows)

    def messages(number, g):
        levels = levels_of(g)
        first = first_messages(g)[number]
        result = []
        if number < len(levels):
            axes, rows, taken, _ = levels[number]
            for n, steps in enumerate(offsets_of(axes, False)):
                start = part_of(axes, steps) * rows
                if number == 0:
                    src = part.at[g, tile_of(start, rows, rows)]
                else:
                    src = kept_sum.at[g, tile_of(levels[number - 1][3] + start, rows, rows)]
                dst = taken_in.at[g, taken + n * rows : taken + (n + 1) * rows]
                result.append((src, dst, steps))
        else:
            level = 2 * len(levels) - 1 - number
            whole = any("y" in axes for axes, _, _, _ in levels[level + 1 :])
            here = state.at[slice(None) if whole else dirs_at, g, state_rows(g, level)]
            result = [(here, here, steps) for steps in offsets_of(levels[level][0], True)]
        return [
            pltpu.make_async_remote_copy(
                src_ref=src,
                dst_ref=dst,
                send_sem=send_sem.at[g, first + n],
                recv_sem=recv_sem.at[g, first + n],
                device_id=device(steps),
                device_id_type=pl.DeviceIdType.MESH,
            )
            for n, (src, dst, steps) in enumerate(result)
        ]

    def stage(number, g):
        levels = levels_of(g)
        depth = len(levels)
        if number > 0:
            for copy in messages(number - 1, g):
                copy.wait()
        if 0 < number <= depth:
            axes, rows, taken, kept = levels[number - 1]
            start = part_of(axes, {}) * rows
            if number == 1:
                total = part[g, tile_of(start, rows, rows), :].astype(F32)
            else:
                total = kept_sum[g, tile_of(levels[number - 2][3] + start, rows, rows), :].astype(F32)
            for n in range(math.prod(SIZE[axis] for axis in axes) - 1):
                total = total + taken_in[g, taken + n * rows : taken + (n + 1) * rows, :].astype(F32)
            if number == depth:
                state[dirs_at, g, state_rows(g, depth - 1), :] = total.astype(BF16)
            else:
                kept_sum[g, kept : kept + rows, :] = total.astype(BF16)
        if number < 2 * depth:
            for copy in messages(number, g):
                copy.start()

    def exchange(t, ticks):
        for tick in ticks:
            if TICKS[tick]:

                @pl.when(t == tick)
                def _(tick=tick):
                    for g, number in TICKS[tick]:
                        stage(number, g)

    dirs_send[...] = jnp.zeros_like(dirs_send)
    dirs_send[0:3, 0:DIRS] = dirs_rows_ref[...]
    for f in range(FREQS):
        freq_tile[f : f + 1, :] = jnp.full((1, 128), freq_ref[f] * (0.5 / math.pi), F32)
    for base, low in ((near_base, 0), (far_base, HALF)):
        columns = tile_of(base, HALF, HALF)
        for axis in range(3):
            pos_tile[axis, :, low : low + HALF] = jnp.broadcast_to(
                pos_ref[axis : axis + 1, columns], (8, HALF)
            )
        alive_tile[:, low : low + HALF] = jnp.broadcast_to(
            jnp.where(domain_ref[:, columns] == atoms_at, 1.0, 0.0), (8, HALF)
        )
    for s in range(gain_ref.shape[0]):
        gain_tile[s] = jnp.broadcast_to(gain_ref[s : s + 1, :], (FEAT, FEAT)).T

    def alive_of(place):
        return jnp.concatenate([alive_tile[:, place]] * (FEAT // 8), axis=0)

    def gain_of(place, columns):
        species = jnp.broadcast_to(species_ref[:, columns], (FEAT, 128))
        gain = gain_tile[0]
        for s in range(1, gain_ref.shape[0]):
            gain = jnp.where(species == s, gain_tile[s], gain)
        return gain * alive_of(place)

    def prepare(block, carry):
        for base, low in ((near_base, 0), (far_base, HALF)):
            columns = tile_of(base + block * 128, 128, 128)
            place = tile_of(low + block * 128, 128, 128)
            keys = k_ref[columns, :].astype(F32).T * gain_of(place, columns)
            key_t[:, place] = keys.astype(BF16)
            query_t[:, place] = (q_ref[columns, :].astype(F32).T * alive_of(place)).astype(BF16)
            if low == 0:
                value_t[:, place] = v_ref[columns, :].astype(F32).T.astype(BF16)
                grad_t[:, place] = g_ref[columns, :].astype(F32).T.astype(BF16)
        return carry

    lax.fori_loop(0, HALF // 128, prepare, 0)

    def coef(u):
        return weight_ref[u] * mask_ref[u].astype(F32) * (1.0 / math.sqrt(FEAT * ATOMS))

    def rotate_to(x_ref, y_ref, u, p, columns, cosine, sine):
        lead = x_ref[p : p + 16, columns]
        trail = x_ref[p + 64 : p + 80, columns]
        y_ref[u, p : p + 16, columns] = lead * cosine - trail * sine
        y_ref[u, p + 64 : p + 80, columns] = lead * sine + trail * cosine

    def angles(dirs, at, columns):
        projected = (
            dirs[0, at] * pos_tile[0, :, columns]
            + dirs[1, at] * pos_tile[1, :, columns]
            + dirs[2, at] * pos_tile[2, :, columns]
        )
        for low_f in range(0, FREQS, 16):
            pairs = []
            for f in (low_f, low_f + 8):
                freq = jnp.concatenate([freq_tile[f : f + 8, :]] * (WIDTH // 128), axis=1)
                pairs.append(cos_sin_turns(projected * freq))
            cosine = jnp.concatenate([pairs[0][0], pairs[1][0]], axis=0).astype(BF16)
            sine = jnp.concatenate([pairs[0][1], pairs[1][1]], axis=0).astype(BF16)
            yield low_f, cosine, sine

    def state_step(i):
        for u in range(GROUP):
            if u == GROUP // 2:
                exchange(2 * i, range(0, 2 * STEPS, 2))
            at = i * GROUP + u
            for low in range(0, ATOMS, WIDTH):
                columns = pl.ds(low, WIDTH)
                for low_f, cosine, sine in angles(dirs_ref, at, columns):
                    if low < HALF:
                        cos_sin[at, 0, low_f : low_f + 16, columns] = cosine
                        cos_sin[at, 1, low_f : low_f + 16, columns] = sine
                    for p in (low_f, low_f + FREQS):
                        rotate_to(key_t, key_rot, u, p, columns, cosine, sine)
                        rotate_to(query_t, query_rot, u, p, columns, cosine, sine)
        for at_row, rotated, rows in ((0, key_rot, v_ref), (ROWS, query_rot, g_ref)):
            product = jnp.zeros((ROWS, FEAT), F32)
            for base, low in ((near_base, 0), (far_base, HALF)):
                product = product + jnp.dot(
                    rotated[:, :, low : low + HALF].reshape(ROWS, HALF),
                    rows[tile_of(base, HALF, HALF), :],
                    preferred_element_type=F32,
                )
            for u in range(GROUP):
                part[i, at_row + u * FEAT : at_row + (u + 1) * FEAT, :] = (
                    product[u * FEAT : (u + 1) * FEAT] * coef(i * GROUP + u)
                ).astype(BF16)

    def far_angles(at):
        for low in range(0, HALF, WIDTH):
            columns = pl.ds(low, WIDTH)
            for low_f, cosine, sine in angles(far_dirs, at, columns):
                cos_sin[DIRS + at, 0, low_f : low_f + 16, columns] = cosine
                cos_sin[DIRS + at, 1, low_f : low_f + 16, columns] = sine

    def output_step(i, far):
        low_at = far * HALF
        table_at = far * DIRS + i * GROUP
        for u in range(GROUP):
            for low in range(0, HALF, WIDTH):
                columns = pl.ds(low, WIDTH)
                place = pl.ds(low_at + low, WIDTH)
                for low_f in range(0, FREQS, 16):
                    cosine = cos_sin[table_at + u, 0, low_f : low_f + 16, columns]
                    sine = cos_sin[table_at + u, 1, low_f : low_f + 16, columns]
                    for p in (low_f, low_f + FREQS):
                        for x_ref, y_ref in ((key_t, key_rot), (query_t, query_rot)):
                            lead = x_ref[p : p + 16, columns]
                            trail = x_ref[p + 64 : p + 80, columns]
                            y_ref[u, p : p + 16, place] = lead * cosine - trail * sine
                            y_ref[u, p + 64 : p + 80, place] = lead * sine + trail * cosine
        owner = 1 - dirs_at if far else dirs_at
        forward = state[owner, i, :ROWS, :]
        backward = state[owner, i, ROWS:, :]
        contract = (((0,), (0,)), ((), ()))
        for matrix, rotated, rows_t, total, back in (
            (forward, query_rot, grad_t, att_acc, back_q),
            (backward, key_rot, value_t, gv_acc, back_k),
        ):
            back[far] = (
                jnp.dot(matrix, rows_t[...], preferred_element_type=F32)
                .astype(BF16)
                .reshape(GROUP, FEAT, HALF)
            )
            total[...] += lax.dot_general(
                matrix,
                rotated[:, :, low_at : low_at + HALF].reshape(ROWS, HALF),
                contract,
                preferred_element_type=F32,
            )
        for low in range(0, HALF, WIDTH):
            columns = pl.ds(low, WIDTH)
            for low_f in range(0, FREQS, 16):
                tables = [
                    cos_sin[table_at + u, :, low_f : low_f + 16, columns] for u in range(GROUP)
                ]
                for p in (low_f, low_f + FREQS):
                    for back, total in ((back_q, gq_acc), (back_k, gk_acc)):
                        lead_sum = trail_sum = None
                        for u in range(GROUP):
                            cosine, sine = tables[u][0], tables[u][1]
                            lead = back[far, u, p : p + 16, columns]
                            trail = back[far, u, p + 64 : p + 80, columns]
                            new_lead = lead * cosine + trail * sine
                            new_trail = trail * cosine - lead * sine
                            lead_sum = new_lead if u == 0 else lead_sum + new_lead
                            trail_sum = new_trail if u == 0 else trail_sum + new_trail
                        total[p : p + 16, columns] += lead_sum.astype(F32)
                        total[p + 64 : p + 80, columns] += trail_sum.astype(F32)

    totals = (att_acc, gq_acc, gk_acc, gv_acc)
    for total in totals:
        total[...] = jnp.zeros_like(total)

    pl.semaphore_wait(barrier, len(partners))

    dirs_copy = pltpu.make_async_remote_copy(
        src_ref=dirs_send,
        dst_ref=dirs_recv,
        send_sem=dirs_sem.at[0],
        recv_sem=dirs_sem.at[1],
        device_id={"dirs": 1 - dirs_at},
        device_id_type=pl.DeviceIdType.MESH,
    )
    dirs_copy.start()

    def first_loop(i, carry):
        state_step(i)
        exchange(2 * i + 1, range(1, 2 * STEPS, 2))
        return carry

    lax.fori_loop(0, STEPS, first_loop, 0)

    dirs_copy.wait()
    to_scalars = pltpu.make_async_copy(dirs_recv, far_dirs, dirs_sem.at[2])
    to_scalars.start()
    to_scalars.wait()

    def fill_loop(t, carry):
        exchange(t + 2 * STEPS, range(2 * STEPS, 2 * STEPS + FILL))

        def fill(n, inner):
            far_angles(t * (DIRS // FILL) + n)
            return inner

        return lax.fori_loop(0, DIRS // FILL, fill, carry)

    lax.fori_loop(0, FILL, fill_loop, 0)

    def second_loop(i, carry):
        at = 2 * STEPS + FILL
        for far in range(2):
            exchange(at + 2 * i + far, range(at + far, at + 2 * STEPS, 2))
            output_step(i, far)
        return carry

    lax.fori_loop(0, STEPS, second_loop, 0)

    def finish(block, carry):
        place = tile_of(block * 128, 128, 128)
        alive = alive_of(place)
        gain = gain_of(place, tile_of(near_base + block * 128, 128, 128))
        for total, out, factor in zip(
            totals, (att_out, gq_out, gk_out, gv_out), (None, alive, gain, None)
        ):
            whole = total[:, place]
            if factor is not None:
                whole = whole * factor
            out[:, place] = whole.astype(BF16)
        return carry

    lax.fori_loop(0, HALF // 128, finish, 0)


def turn_kernel(*refs):
    def turn(block, carry):
        rows = tile_of(block * 128, 128, 128)
        for source, result in zip(refs[:4], refs[4:]):
            result[rows, :] = source[:, rows].astype(F32).T.astype(BF16)
        return carry

    lax.fori_loop(0, HALF // 128, turn, 0)


def per_device(
    queries,
    keys,
    values,
    cotangent,
    positions,
    species,
    domain,
    species_gain,
    frequency,
    directions,
    dir_weight,
    dir_mask,
):
    smem = pl.BlockSpec(memory_space=pltpu.SMEM)
    vmem = pl.BlockSpec(memory_space=pltpu.VMEM)
    species_count = species_gain.shape[0]
    scratch = [
        pltpu.VMEM((FREQS, 128), F32),
        pltpu.VMEM((3, 8, ATOMS), F32),
        pltpu.VMEM((species_count, FEAT, FEAT), F32),
        pltpu.VMEM((8, ATOMS), F32),
        pltpu.VMEM((FEAT, ATOMS), BF16),
        pltpu.VMEM((FEAT, ATOMS), BF16),
        pltpu.VMEM((FEAT, HALF), BF16),
        pltpu.VMEM((FEAT, HALF), BF16),
        pltpu.VMEM((2 * DIRS, 2, FREQS, HALF), BF16),
        pltpu.VMEM((GROUP, FEAT, ATOMS), BF16),
        pltpu.VMEM((GROUP, FEAT, ATOMS), BF16),
        pltpu.VMEM((2, GROUP, FEAT, HALF), BF16),
        pltpu.VMEM((2, GROUP, FEAT, HALF), BF16),
        pltpu.VMEM((FEAT, HALF), F32),
        pltpu.VMEM((FEAT, HALF), F32),
        pltpu.VMEM((FEAT, HALF), F32),
        pltpu.VMEM((FEAT, HALF), F32),
        pltpu.VMEM((STEPS, 2 * ROWS, FEAT), BF16),
        pltpu.VMEM((STEPS, 2 * ROWS, FEAT), BF16),
        pltpu.VMEM((STEPS, 2 * ROWS, FEAT), BF16),
        pltpu.VMEM((2, STEPS, 2 * ROWS, FEAT), BF16),
        pltpu.VMEM((8, 128), F32),
        pltpu.VMEM((8, 128), F32),
        pltpu.SMEM((8, 128), F32),
        pltpu.SemaphoreType.DMA((STEPS, MESSAGES)),
        pltpu.SemaphoreType.DMA((STEPS, MESSAGES)),
        pltpu.SemaphoreType.DMA((3,)),
    ]
    turned = pl.pallas_call(
        kernel,
        out_shape=[jax.ShapeDtypeStruct((FEAT, HALF), BF16)] * 4,
        in_specs=[smem] * 4 + [vmem] * 9,
        out_specs=[vmem] * 4,
        scratch_shapes=scratch,
        compiler_params=pltpu.CompilerParams(
            collective_id=0, has_side_effects=True, vmem_limit_bytes=56 * 2**20
        ),
        name="fast_attention",
    )(
        frequency,
        directions,
        dir_weight,
        dir_mask,
        directions,
        queries,
        keys,
        values,
        cotangent,
        positions,
        species.reshape(1, ATOMS),
        domain.reshape(1, ATOMS),
        species_gain,
    )
    return tuple(
        pl.pallas_call(
            turn_kernel,
            out_shape=[jax.ShapeDtypeStruct((HALF, FEAT), BF16)] * 4,
            in_specs=[vmem] * 4,
            out_specs=[vmem] * 4,
            name="turn_results",
        )(*turned)
    )


def solution(mesh):
    return jax.shard_map(
        per_device,
        mesh=mesh,
        in_specs=(
            P("atoms", None),
            P("atoms", None),
            P("atoms", None),
            P("atoms", None),
            P(None, "atoms"),
            P("atoms"),
            P("atoms"),
            P(),
            P(),
            P(None, "dirs"),
            P("dirs"),
            P("dirs"),
        ),
        out_specs=(
            P(("atoms", "dirs"), None),
            P(("atoms", "dirs"), None),
            P(("atoms", "dirs"), None),
            P(("atoms", "dirs"), None),
        ),
        check_vma=False,
    )
```

```python
import itertools
import math

import jax
import jax.numpy as jnp
from jax import lax
from jax.experimental import pallas as pl
from jax.experimental.pallas import tpu as pltpu
from jax.sharding import PartitionSpec as P

F32 = jnp.float32
BF16 = jnp.bfloat16

ATOMS = 2048
HALF = ATOMS // 2
FEAT = 128
FREQS = 32
DIRS = 44
GROUP = 4
STEPS = DIRS // GROUP
ROWS = GROUP * FEAT
WIDTH = 256

SINE = (4.4428795675460835, -7.307816684491783, 3.59777417808721, -0.791199392161295)
COSINE = (1.4142040148090755, -6.977637323456294, 5.715187874756719, -1.7282138922235275)

ORDERS = (('x', 'y', 'z'), ('z', 'y', 'x'))
SIZE = {"c": 2, "x": 4, "z": 4, "y": 2}
STAGES = 9
FILL = 4
TICKS = (
    (),
    ((0, 0),),
    (),
    ((0, 1), (1, 0)),
    (),
    ((1, 1), (2, 0)),
    (),
    ((2, 1), (3, 0)),
    ((0, 2),),
    ((3, 1), (4, 0)),
    ((1, 2),),
    ((4, 1), (5, 0)),
    ((0, 3), (2, 2)),
    ((5, 1), (6, 0)),
    ((1, 3), (3, 2)),
    ((6, 1), (7, 0)),
    ((0, 4), (2, 3), (4, 2)),
    ((7, 1), (8, 0)),
    ((1, 4), (3, 3), (5, 2)),
    ((0, 5), (6, 2), (8, 1), (9, 0)),
    ((2, 4), (4, 3)),
    ((1, 5), (3, 4), (7, 2), (9, 1), (10, 0)),
    ((5, 3),),
    ((0, 6), (6, 3), (10, 1)),
    ((2, 5), (3, 5), (4, 4), (8, 2)),
    ((1, 6), (5, 4), (7, 3), (9, 2)),
    ((6, 4), (4, 5), (2, 6), (0, 7), (3, 6), (8, 3), (9, 3), (10, 2), (5, 5), (7, 4), (0, 8)),
    ((1, 7), (4, 6), (6, 5)),
    ((10, 3), (2, 7), (9, 4), (1, 8)),
    ((3, 7), (5, 6), (7, 5), (8, 4)),
    ((2, 8), (6, 6), (10, 4)),
    ((3, 8), (4, 7), (9, 5)),
    ((7, 6),),
    ((4, 8), (5, 7), (8, 5), (10, 5)),
    ((6, 7), (9, 6)),
    ((5, 8),),
    ((6, 8), (7, 7), (8, 6), (10, 6)),
    (),
    ((7, 8),),
    ((9, 7),),
    (),
    ((8, 7), (9, 8)),
    ((10, 7), (8, 8)),
    (),
    ((10, 8),),
    (),
    (),
    (),
)


def levels_of(g):
    levels, rows, taken, kept = [], 2 * ROWS, 0, 0
    for axes in ("c",) + ORDERS[g % len(ORDERS)]:
        count = math.prod(SIZE[axis] for axis in axes)
        rows //= count
        levels.append((axes, rows, taken, kept))
        taken += (count - 1) * rows
        kept += rows
    return levels


def offsets_of(axes, gather):
    choices = []
    for axis in axes:
        if gather and axis == "y":
            choices.append([{"y": h, "d": d} for h in range(2) for d in range(2)])
        else:
            choices.append([{axis: step} for step in range(SIZE[axis])])
    merged = [{k: v for part in parts for k, v in part.items()} for parts in itertools.product(*choices)]
    return [steps for steps in merged if any(steps.values())]


def horner(coefficients, square):
    total = square * coefficients[-1] + coefficients[-2]
    for coefficient in coefficients[-3::-1]:
        total = total * square + coefficient
    return total


def cos_sin_turns(turns):
    rest = turns - jnp.round(turns)
    square = rest * rest
    sine = horner(SINE, square) * rest
    cosine = horner(COSINE, square)
    return 1.0 - sine * sine, sine * cosine


def tile_of(start, size, unit):
    return pl.ds(pl.multiple_of(start, unit), size)


def kernel(
    freq_ref,
    dirs_ref,
    weight_ref,
    mask_ref,
    dirs_rows_ref,
    q_ref,
    k_ref,
    v_ref,
    g_ref,
    pos_ref,
    species_ref,
    domain_ref,
    gain_ref,
    att_out,
    gq_out,
    gk_out,
    gv_out,
    freq_tile,
    pos_tile,
    gain_tile,
    alive_tile,
    key_t,
    query_t,
    value_t,
    grad_t,
    cos_sin,
    key_rot,
    query_rot,
    back_q,
    back_k,
    att_acc,
    gv_acc,
    gq_acc,
    gk_acc,
    part,
    taken_in,
    kept_sum,
    state,
    dirs_send,
    dirs_recv,
    far_dirs,
    send_sem,
    recv_sem,
    dirs_sem,
):
    atoms_at = lax.axis_index("atoms")
    dirs_at = lax.axis_index("dirs")
    core = lax.rem(atoms_at, 2)
    z_at = lax.rem(lax.div(atoms_at, 2), 4)
    x_at = lax.rem(lax.div(atoms_at, 8), 4)
    y_at = lax.div(atoms_at, 32)
    near_base = dirs_at * HALF
    far_base = HALF - near_base

    place = {"c": core, "x": x_at, "z": z_at, "y": y_at}

    def device(steps):
        at = {axis: lax.rem(place[axis] + steps.get(axis, 0), SIZE[axis]) for axis in place}
        to = {"atoms": ((at["y"] * 4 + at["x"]) * 4 + at["z"]) * 2 + at["c"]}
        if steps.get("d", 0):
            to["dirs"] = 1 - dirs_at
        return to

    def part_of(axes, steps):
        index = 0
        for axis in axes:
            index = index * SIZE[axis] + lax.rem(place[axis] + steps.get(axis, 0), SIZE[axis])
        return index

    met = []
    for g in range(STEPS):
        for axes, _, _, _ in levels_of(g):
            met += [steps for steps in offsets_of(axes, True) if steps not in met]
    met += [steps for steps in ({"d": 1},) if {"y": 0, "d": 1} not in met]
    barrier = pltpu.get_barrier_semaphore()
    partners = [device(steps) for steps in met]
    for partner in partners:
        pl.semaphore_signal(
            barrier, inc=1, device_id=partner, device_id_type=pl.DeviceIdType.MESH
        )

    def state_rows(g, level):
        start = 0
        for axes, rows, _, _ in levels_of(g)[: level + 1]:
            start = start + part_of(axes, {}) * rows
        rows = levels_of(g)[level][1]
        return tile_of(start, rows, rows)

    def messages(number, g):
        levels = levels_of(g)
        result = []
        if number < len(levels):
            axes, rows, taken, _ = levels[number]
            for n, steps in enumerate(offsets_of(axes, False)):
                start = part_of(axes, steps) * rows
                if number == 0:
                    src = part.at[g, tile_of(start, rows, rows)]
                else:
                    src = kept_sum.at[g, tile_of(levels[number - 1][3] + start, rows, rows)]
                dst = taken_in.at[g, taken + n * rows : taken + (n + 1) * rows]
                result.append((src, dst, steps))
        else:
            level = 2 * len(levels) - 1 - number
            whole = any("y" in axes for axes, _, _, _ in levels[level + 1 :])
            here = state.at[slice(None) if whole else dirs_at, g, state_rows(g, level)]
            result = [(here, here, steps) for steps in offsets_of(levels[level][0], True)]
        return [
            pltpu.make_async_remote_copy(
                src_ref=src,
                dst_ref=dst,
                send_sem=send_sem.at[g, number],
                recv_sem=recv_sem.at[g, number],
                device_id=device(steps),
                device_id_type=pl.DeviceIdType.MESH,
            )
            for src, dst, steps in result
        ]

    def all_bytes(number, g):
        levels = levels_of(g)
        if number < len(levels):
            axes, rows, taken, _ = levels[number]
            return taken_in.at[g, taken : taken + len(offsets_of(axes, False)) * rows]
        level = 2 * len(levels) - 1 - number
        axes, rows, _, _ = levels[level]
        whole = any("y" in others for others, _, _, _ in levels[level + 1 :])
        return state.at[slice(None) if whole else 0, g, : len(offsets_of(axes, True)) * rows]

    def stage(number, g):
        levels = levels_of(g)
        depth = len(levels)
        if number > 0:
            total = all_bytes(number - 1, g)
            for sem in (send_sem, recv_sem):
                pltpu.make_async_copy(total, total, sem.at[g, number - 1]).wait()
        if 0 < number <= depth:
            axes, rows, taken, kept = levels[number - 1]
            start = part_of(axes, {}) * rows
            if number == 1:
                total = part[g, tile_of(start, rows, rows), :].astype(F32)
            else:
                total = kept_sum[g, tile_of(levels[number - 2][3] + start, rows, rows), :].astype(F32)
            for n in range(math.prod(SIZE[axis] for axis in axes) - 1):
                total = total + taken_in[g, taken + n * rows : taken + (n + 1) * rows, :].astype(F32)
            if number == depth:
                state[dirs_at, g, state_rows(g, depth - 1), :] = total.astype(BF16)
            else:
                kept_sum[g, kept : kept + rows, :] = total.astype(BF16)
        if number < 2 * depth:
            for copy in messages(number, g):
                copy.start()

    def exchange(t, ticks):
        for tick in ticks:
            if TICKS[tick]:

                @pl.when(t == tick)
                def _(tick=tick):
                    for g, number in TICKS[tick]:
                        stage(number, g)

    dirs_send[...] = jnp.zeros_like(dirs_send)
    dirs_send[0:3, 0:DIRS] = dirs_rows_ref[...]
    for f in range(FREQS):
        freq_tile[f : f + 1, :] = jnp.full((1, 128), freq_ref[f] * (0.5 / math.pi), F32)
    for base, low in ((near_base, 0), (far_base, HALF)):
        columns = tile_of(base, HALF, HALF)
        for axis in range(3):
            pos_tile[axis, :, low : low + HALF] = jnp.broadcast_to(
                pos_ref[axis : axis + 1, columns], (8, HALF)
            )
        alive_tile[:, low : low + HALF] = jnp.broadcast_to(
            jnp.where(domain_ref[:, columns] == atoms_at, 1.0, 0.0), (8, HALF)
        )
    for s in range(gain_ref.shape[0]):
        gain_tile[s] = jnp.broadcast_to(gain_ref[s : s + 1, :], (FEAT, FEAT)).T

    def alive_of(place):
        return jnp.concatenate([alive_tile[:, place]] * (FEAT // 8), axis=0)

    def gain_of(place, columns):
        species = jnp.broadcast_to(species_ref[:, columns], (FEAT, 128))
        gain = gain_tile[0]
        for s in range(1, gain_ref.shape[0]):
            gain = jnp.where(species == s, gain_tile[s], gain)
        return gain * alive_of(place)

    def prepare(block, carry):
        for base, low in ((near_base, 0), (far_base, HALF)):
            columns = tile_of(base + block * 128, 128, 128)
            place = tile_of(low + block * 128, 128, 128)
            keys = k_ref[columns, :].astype(F32).T * gain_of(place, columns)
            key_t[:, place] = keys.astype(BF16)
            query_t[:, place] = (q_ref[columns, :].astype(F32).T * alive_of(place)).astype(BF16)
            if low == 0:
                value_t[:, place] = v_ref[columns, :].astype(F32).T.astype(BF16)
                grad_t[:, place] = g_ref[columns, :].astype(F32).T.astype(BF16)
        return carry

    lax.fori_loop(0, HALF // 128, prepare, 0)

    def coef(u):
        return weight_ref[u] * mask_ref[u].astype(F32) * (1.0 / math.sqrt(FEAT * ATOMS))

    def rotate_to(x_ref, y_ref, u, p, columns, cosine, sine):
        lead = x_ref[p : p + 16, columns]
        trail = x_ref[p + 64 : p + 80, columns]
        y_ref[u, p : p + 16, columns] = lead * cosine - trail * sine
        y_ref[u, p + 64 : p + 80, columns] = lead * sine + trail * cosine

    def angles(dirs, at, columns):
        projected = (
            dirs[0, at] * pos_tile[0, :, columns]
            + dirs[1, at] * pos_tile[1, :, columns]
            + dirs[2, at] * pos_tile[2, :, columns]
        )
        for low_f in range(0, FREQS, 16):
            pairs = []
            for f in (low_f, low_f + 8):
                freq = jnp.concatenate([freq_tile[f : f + 8, :]] * (WIDTH // 128), axis=1)
                pairs.append(cos_sin_turns(projected * freq))
            cosine = jnp.concatenate([pairs[0][0], pairs[1][0]], axis=0).astype(BF16)
            sine = jnp.concatenate([pairs[0][1], pairs[1][1]], axis=0).astype(BF16)
            yield low_f, cosine, sine

    def state_step(i):
        for u in range(GROUP):
            if u == GROUP // 2:
                exchange(2 * i, range(0, 2 * STEPS, 2))
            at = i * GROUP + u
            for low in range(0, ATOMS, WIDTH):
                columns = pl.ds(low, WIDTH)
                for low_f, cosine, sine in angles(dirs_ref, at, columns):
                    if low < HALF:
                        cos_sin[at, 0, low_f : low_f + 16, columns] = cosine
                        cos_sin[at, 1, low_f : low_f + 16, columns] = sine
                    for p in (low_f, low_f + FREQS):
                        rotate_to(key_t, key_rot, u, p, columns, cosine, sine)
                        rotate_to(query_t, query_rot, u, p, columns, cosine, sine)
        for at_row, rotated, rows in ((0, key_rot, v_ref), (ROWS, query_rot, g_ref)):
            product = jnp.zeros((ROWS, FEAT), F32)
            for base, low in ((near_base, 0), (far_base, HALF)):
                product = product + jnp.dot(
                    rotated[:, :, low : low + HALF].reshape(ROWS, HALF),
                    rows[tile_of(base, HALF, HALF), :],
                    preferred_element_type=F32,
                )
            for u in range(GROUP):
                part[i, at_row + u * FEAT : at_row + (u + 1) * FEAT, :] = (
                    product[u * FEAT : (u + 1) * FEAT] * coef(i * GROUP + u)
                ).astype(BF16)

    def far_angles(at):
        for low in range(0, HALF, WIDTH):
            columns = pl.ds(low, WIDTH)
            for low_f, cosine, sine in angles(far_dirs, at, columns):
                cos_sin[DIRS + at, 0, low_f : low_f + 16, columns] = cosine
                cos_sin[DIRS + at, 1, low_f : low_f + 16, columns] = sine

    def output_step(i, far):
        low_at = far * HALF
        table_at = far * DIRS + i * GROUP
        for u in range(GROUP):
            for low in range(0, HALF, WIDTH):
                columns = pl.ds(low, WIDTH)
                place = pl.ds(low_at + low, WIDTH)
                for low_f in range(0, FREQS, 16):
                    cosine = cos_sin[table_at + u, 0, low_f : low_f + 16, columns]
                    sine = cos_sin[table_at + u, 1, low_f : low_f + 16, columns]
                    for p in (low_f, low_f + FREQS):
                        for x_ref, y_ref in ((key_t, key_rot), (query_t, query_rot)):
                            lead = x_ref[p : p + 16, columns]
                            trail = x_ref[p + 64 : p + 80, columns]
                            y_ref[u, p : p + 16, place] = lead * cosine - trail * sine
                            y_ref[u, p + 64 : p + 80, place] = lead * sine + trail * cosine
        owner = 1 - dirs_at if far else dirs_at
        forward = state[owner, i, :ROWS, :]
        backward = state[owner, i, ROWS:, :]
        contract = (((0,), (0,)), ((), ()))
        for matrix, rotated, rows_t, total, back in (
            (forward, query_rot, grad_t, att_acc, back_q),
            (backward, key_rot, value_t, gv_acc, back_k),
        ):
            back[far] = (
                jnp.dot(matrix, rows_t[...], preferred_element_type=F32)
                .astype(BF16)
                .reshape(GROUP, FEAT, HALF)
            )
            total[...] += lax.dot_general(
                matrix,
                rotated[:, :, low_at : low_at + HALF].reshape(ROWS, HALF),
                contract,
                preferred_element_type=F32,
            )
        for low in range(0, HALF, WIDTH):
            columns = pl.ds(low, WIDTH)
            for low_f in range(0, FREQS, 16):
                tables = [
                    cos_sin[table_at + u, :, low_f : low_f + 16, columns] for u in range(GROUP)
                ]
                for p in (low_f, low_f + FREQS):
                    for back, total in ((back_q, gq_acc), (back_k, gk_acc)):
                        lead_sum = trail_sum = None
                        for u in range(GROUP):
                            cosine, sine = tables[u][0], tables[u][1]
                            lead = back[far, u, p : p + 16, columns]
                            trail = back[far, u, p + 64 : p + 80, columns]
                            new_lead = lead * cosine + trail * sine
                            new_trail = trail * cosine - lead * sine
                            lead_sum = new_lead if u == 0 else lead_sum + new_lead
                            trail_sum = new_trail if u == 0 else trail_sum + new_trail
                        total[p : p + 16, columns] += lead_sum.astype(F32)
                        total[p + 64 : p + 80, columns] += trail_sum.astype(F32)

    totals = (att_acc, gq_acc, gk_acc, gv_acc)
    for total in totals:
        total[...] = jnp.zeros_like(total)

    pl.semaphore_wait(barrier, len(partners))

    dirs_copy = pltpu.make_async_remote_copy(
        src_ref=dirs_send,
        dst_ref=dirs_recv,
        send_sem=dirs_sem.at[0],
        recv_sem=dirs_sem.at[1],
        device_id={"dirs": 1 - dirs_at},
        device_id_type=pl.DeviceIdType.MESH,
    )
    dirs_copy.start()

    def first_loop(i, carry):
        state_step(i)
        exchange(2 * i + 1, range(1, 2 * STEPS, 2))
        return carry

    lax.fori_loop(0, STEPS, first_loop, 0)

    dirs_copy.wait()
    to_scalars = pltpu.make_async_copy(dirs_recv, far_dirs, dirs_sem.at[2])
    to_scalars.start()
    to_scalars.wait()

    def fill_loop(t, carry):
        exchange(t + 2 * STEPS, range(2 * STEPS, 2 * STEPS + FILL))

        def fill(n, inner):
            far_angles(t * (DIRS // FILL) + n)
            return inner

        return lax.fori_loop(0, DIRS // FILL, fill, carry)

    lax.fori_loop(0, FILL, fill_loop, 0)

    def second_loop(i, carry):
        at = 2 * STEPS + FILL
        for far in range(2):
            exchange(at + 2 * i + far, range(at + far, at + 2 * STEPS, 2))
            output_step(i, far)
        return carry

    lax.fori_loop(0, STEPS, second_loop, 0)

    def finish(block, carry):
        place = tile_of(block * 128, 128, 128)
        alive = alive_of(place)
        gain = gain_of(place, tile_of(near_base + block * 128, 128, 128))
        for total, out, factor in zip(
            totals, (att_out, gq_out, gk_out, gv_out), (None, alive, gain, None)
        ):
            whole = total[:, place]
            if factor is not None:
                whole = whole * factor
            out[:, place] = whole.astype(BF16)
        return carry

    lax.fori_loop(0, HALF // 128, finish, 0)


def turn_kernel(*refs):
    def turn(block, carry):
        rows = tile_of(block * 128, 128, 128)
        for source, result in zip(refs[:4], refs[4:]):
            result[rows, :] = source[:, rows].T
        return carry

    lax.fori_loop(0, HALF // 128, turn, 0)


def per_device(
    queries,
    keys,
    values,
    cotangent,
    positions,
    species,
    domain,
    species_gain,
    frequency,
    directions,
    dir_weight,
    dir_mask,
):
    smem = pl.BlockSpec(memory_space=pltpu.SMEM)
    vmem = pl.BlockSpec(memory_space=pltpu.VMEM)
    species_count = species_gain.shape[0]
    scratch = [
        pltpu.VMEM((FREQS, 128), F32),
        pltpu.VMEM((3, 8, ATOMS), F32),
        pltpu.VMEM((species_count, FEAT, FEAT), F32),
        pltpu.VMEM((8, ATOMS), F32),
        pltpu.VMEM((FEAT, ATOMS), BF16),
        pltpu.VMEM((FEAT, ATOMS), BF16),
        pltpu.VMEM((FEAT, HALF), BF16),
        pltpu.VMEM((FEAT, HALF), BF16),
        pltpu.VMEM((2 * DIRS, 2, FREQS, HALF), BF16),
        pltpu.VMEM((GROUP, FEAT, ATOMS), BF16),
        pltpu.VMEM((GROUP, FEAT, ATOMS), BF16),
        pltpu.VMEM((2, GROUP, FEAT, HALF), BF16),
        pltpu.VMEM((2, GROUP, FEAT, HALF), BF16),
        pltpu.VMEM((FEAT, HALF), F32),
        pltpu.VMEM((FEAT, HALF), F32),
        pltpu.VMEM((FEAT, HALF), F32),
        pltpu.VMEM((FEAT, HALF), F32),
        pltpu.VMEM((STEPS, 2 * ROWS, FEAT), BF16),
        pltpu.VMEM((STEPS, 2 * ROWS, FEAT), BF16),
        pltpu.VMEM((STEPS, 2 * ROWS, FEAT), BF16),
        pltpu.VMEM((2, STEPS, 2 * ROWS, FEAT), BF16),
        pltpu.VMEM((8, 128), F32),
        pltpu.VMEM((8, 128), F32),
        pltpu.SMEM((8, 128), F32),
        pltpu.SemaphoreType.DMA((STEPS, STAGES - 1)),
        pltpu.SemaphoreType.DMA((STEPS, STAGES - 1)),
        pltpu.SemaphoreType.DMA((3,)),
    ]
    turned = pl.pallas_call(
        kernel,
        out_shape=[jax.ShapeDtypeStruct((FEAT, HALF), BF16)] * 4,
        in_specs=[smem] * 4 + [vmem] * 9,
        out_specs=[vmem] * 4,
        scratch_shapes=scratch,
        compiler_params=pltpu.CompilerParams(
            collective_id=0, has_side_effects=True, vmem_limit_bytes=56 * 2**20
        ),
        name="fast_attention",
    )(
        frequency,
        directions,
        dir_weight,
        dir_mask,
        directions,
        queries,
        keys,
        values,
        cotangent,
        positions,
        species.reshape(1, ATOMS),
        domain.reshape(1, ATOMS),
        species_gain,
    )
    return tuple(
        pl.pallas_call(
            turn_kernel,
            out_shape=[jax.ShapeDtypeStruct((HALF, FEAT), BF16)] * 4,
            in_specs=[vmem] * 4,
            out_specs=[vmem] * 4,
            name="turn_results",
        )(*turned)
    )


def solution(mesh):
    return jax.shard_map(
        per_device,
        mesh=mesh,
        in_specs=(
            P("atoms", None),
            P("atoms", None),
            P("atoms", None),
            P("atoms", None),
            P(None, "atoms"),
            P("atoms"),
            P("atoms"),
            P(),
            P(),
            P(None, "dirs"),
            P("dirs"),
            P("dirs"),
        ),
        out_specs=(
            P(("atoms", "dirs"), None),
            P(("atoms", "dirs"), None),
            P(("atoms", "dirs"), None),
            P(("atoms", "dirs"), None),
        ),
        check_vma=False,
    )
```

```python
import itertools
import math

import jax
import jax.numpy as jnp
from jax import lax
from jax.experimental import pallas as pl
from jax.experimental.pallas import tpu as pltpu
from jax.sharding import PartitionSpec as P

F32 = jnp.float32
BF16 = jnp.bfloat16

ATOMS = 2048
HALF = ATOMS // 2
FEAT = 128
FREQS = 32
DIRS = 44
GROUP = 4
STEPS = DIRS // GROUP
ROWS = GROUP * FEAT
WIDTH = 256

SINE = (4.4428795675460835, -7.307816684491783, 3.59777417808721, -0.791199392161295)
COSINE = (1.4142040148090755, -6.977637323456294, 5.715187874756719, -1.7282138922235275)

ORDERS = (('x', 'y', 'z'), ('z', 'y', 'x'))
SIZE = {"c": 2, "x": 4, "z": 4, "y": 2}
STAGES = 9
FILL = 4
TICKS = (
    (),
    ((0, 0),),
    (),
    ((0, 1), (1, 0)),
    (),
    ((1, 1), (2, 0)),
    (),
    ((2, 1), (3, 0)),
    ((0, 2),),
    ((3, 1), (4, 0)),
    ((1, 2),),
    ((4, 1), (5, 0)),
    ((0, 3), (2, 2)),
    ((5, 1), (6, 0)),
    ((1, 3), (3, 2)),
    ((6, 1), (7, 0)),
    ((0, 4), (2, 3), (4, 2)),
    ((7, 1), (8, 0)),
    ((1, 4), (3, 3), (5, 2)),
    ((0, 5), (6, 2), (8, 1), (9, 0)),
    ((2, 4), (4, 3)),
    ((1, 5), (3, 4), (7, 2), (9, 1), (10, 0)),
    ((5, 3),),
    ((0, 6), (6, 3), (10, 1)),
    ((2, 5), (3, 5), (4, 4), (8, 2)),
    ((1, 6), (5, 4), (7, 3), (9, 2)),
    ((6, 4), (4, 5), (2, 6), (0, 7), (3, 6), (8, 3), (9, 3), (10, 2), (5, 5), (7, 4), (0, 8)),
    ((1, 7), (4, 6), (6, 5)),
    ((10, 3), (2, 7), (9, 4), (1, 8)),
    ((3, 7), (5, 6), (7, 5), (8, 4)),
    ((2, 8), (6, 6), (10, 4)),
    ((3, 8), (4, 7), (9, 5)),
    ((7, 6),),
    ((4, 8), (5, 7), (8, 5), (10, 5)),
    ((6, 7), (9, 6)),
    ((5, 8),),
    ((6, 8), (7, 7), (8, 6), (10, 6)),
    (),
    ((7, 8),),
    ((9, 7),),
    (),
    ((8, 7), (9, 8)),
    ((10, 7), (8, 8)),
    (),
    ((10, 8),),
    (),
    (),
    (),
)


def levels_of(g):
    levels, rows, taken, kept = [], 2 * ROWS, 0, 0
    for axes in ("c",) + ORDERS[g % len(ORDERS)]:
        count = math.prod(SIZE[axis] for axis in axes)
        rows //= count
        levels.append((axes, rows, taken, kept))
        taken += (count - 1) * rows
        kept += rows
    return levels


def offsets_of(axes, gather):
    choices = []
    for axis in axes:
        if gather and axis == "y":
            choices.append([{"y": h, "d": d} for h in range(2) for d in range(2)])
        else:
            choices.append([{axis: step} for step in range(SIZE[axis])])
    merged = [{k: v for part in parts for k, v in part.items()} for parts in itertools.product(*choices)]
    return [steps for steps in merged if any(steps.values())]


def horner(coefficients, square):
    total = square * coefficients[-1] + coefficients[-2]
    for coefficient in coefficients[-3::-1]:
        total = total * square + coefficient
    return total


def cos_sin_turns(turns):
    rest = turns - jnp.round(turns)
    square = rest * rest
    sine = horner(SINE, square) * rest
    cosine = horner(COSINE, square)
    return 1.0 - sine * sine, sine * cosine


def tile_of(start, size, unit):
    return pl.ds(pl.multiple_of(start, unit), size)


def kernel(
    freq_ref,
    dirs_ref,
    weight_ref,
    mask_ref,
    dirs_rows_ref,
    q_ref,
    k_ref,
    v_ref,
    g_ref,
    pos_ref,
    species_ref,
    domain_ref,
    gain_ref,
    att_out,
    gq_out,
    gk_out,
    gv_out,
    freq_tile,
    pos_tile,
    gain_tile,
    alive_tile,
    key_t,
    query_t,
    value_t,
    grad_t,
    cos_sin,
    key_rot,
    query_rot,
    back_q,
    back_k,
    att_acc,
    gv_acc,
    gq_acc,
    gk_acc,
    part,
    taken_in,
    kept_sum,
    state,
    dirs_send,
    dirs_recv,
    far_dirs,
    send_sem,
    recv_sem,
    dirs_sem,
):
    atoms_at = lax.axis_index("atoms")
    dirs_at = lax.axis_index("dirs")
    core = lax.rem(atoms_at, 2)
    z_at = lax.rem(lax.div(atoms_at, 2), 4)
    x_at = lax.rem(lax.div(atoms_at, 8), 4)
    y_at = lax.div(atoms_at, 32)
    near_base = dirs_at * HALF
    far_base = HALF - near_base

    place = {"c": core, "x": x_at, "z": z_at, "y": y_at}

    def device(steps):
        at = {axis: lax.rem(place[axis] + steps.get(axis, 0), SIZE[axis]) for axis in place}
        to = {"atoms": ((at["y"] * 4 + at["x"]) * 4 + at["z"]) * 2 + at["c"]}
        if steps.get("d", 0):
            to["dirs"] = 1 - dirs_at
        return to

    def part_of(axes, steps):
        index = 0
        for axis in axes:
            index = index * SIZE[axis] + lax.rem(place[axis] + steps.get(axis, 0), SIZE[axis])
        return index

    met = []
    for g in range(STEPS):
        for axes, _, _, _ in levels_of(g):
            met += [steps for steps in offsets_of(axes, True) if steps not in met]
    met += [steps for steps in ({"d": 1},) if {"y": 0, "d": 1} not in met]
    barrier = pltpu.get_barrier_semaphore()
    partners = [device(steps) for steps in met]
    for partner in partners:
        pl.semaphore_signal(
            barrier, inc=1, device_id=partner, device_id_type=pl.DeviceIdType.MESH
        )

    def state_rows(g, level):
        start = 0
        for axes, rows, _, _ in levels_of(g)[: level + 1]:
            start = start + part_of(axes, {}) * rows
        rows = levels_of(g)[level][1]
        return tile_of(start, rows, rows)

    def messages(number, g):
        levels = levels_of(g)
        result = []
        if number < len(levels):
            axes, rows, taken, _ = levels[number]
            for n, steps in enumerate(offsets_of(axes, False)):
                start = part_of(axes, steps) * rows
                if number == 0:
                    src = part.at[g, tile_of(start, rows, rows)]
                else:
                    src = kept_sum.at[g, tile_of(levels[number - 1][3] + start, rows, rows)]
                dst = taken_in.at[g, taken + n * rows : taken + (n + 1) * rows]
                result.append((src, dst, steps))
        else:
            level = 2 * len(levels) - 1 - number
            whole = any("y" in axes for axes, _, _, _ in levels[level + 1 :])
            here = state.at[slice(None) if whole else dirs_at, g, state_rows(g, level)]
            result = [(here, here, steps) for steps in offsets_of(levels[level][0], True)]
        return [
            pltpu.make_async_remote_copy(
                src_ref=src,
                dst_ref=dst,
                send_sem=send_sem.at[g, number],
                recv_sem=recv_sem.at[g, number],
                device_id=device(steps),
                device_id_type=pl.DeviceIdType.MESH,
            )
            for src, dst, steps in result
        ]

    def all_bytes(number, g):
        levels = levels_of(g)
        if number < len(levels):
            axes, rows, taken, _ = levels[number]
            return taken_in.at[g, taken : taken + len(offsets_of(axes, False)) * rows]
        level = 2 * len(levels) - 1 - number
        axes, rows, _, _ = levels[level]
        whole = any("y" in others for others, _, _, _ in levels[level + 1 :])
        return state.at[slice(None) if whole else 0, g, : len(offsets_of(axes, True)) * rows]

    def stage(number, g):
        levels = levels_of(g)
        depth = len(levels)
        if number > 0:
            total = all_bytes(number - 1, g)
            for sem in (send_sem, recv_sem):
                pltpu.make_async_copy(total, total, sem.at[g, number - 1]).wait()
        if 0 < number <= depth:
            axes, rows, taken, kept = levels[number - 1]
            start = part_of(axes, {}) * rows
            if number == 1:
                total = part[g, tile_of(start, rows, rows), :].astype(F32)
            else:
                total = kept_sum[g, tile_of(levels[number - 2][3] + start, rows, rows), :].astype(F32)
            for n in range(math.prod(SIZE[axis] for axis in axes) - 1):
                total = total + taken_in[g, taken + n * rows : taken + (n + 1) * rows, :].astype(F32)
            if number == depth:
                state[dirs_at, g, state_rows(g, depth - 1), :] = total.astype(BF16)
            else:
                kept_sum[g, kept : kept + rows, :] = total.astype(BF16)
        if number < 2 * depth:
            for copy in messages(number, g):
                copy.start()

    def exchange(t, ticks):
        for tick in ticks:
            if TICKS[tick]:

                @pl.when(t == tick)
                def _(tick=tick):
                    for g, number in TICKS[tick]:
                        stage(number, g)

    dirs_send[...] = jnp.zeros_like(dirs_send)
    dirs_send[0:3, 0:DIRS] = dirs_rows_ref[...]
    for f in range(FREQS):
        freq_tile[f : f + 1, :] = jnp.full((1, 128), freq_ref[f] * (0.5 / math.pi), F32)
    for base, low in ((near_base, 0), (far_base, HALF)):
        columns = tile_of(base, HALF, HALF)
        for axis in range(3):
            pos_tile[axis, :, low : low + HALF] = jnp.broadcast_to(
                pos_ref[axis : axis + 1, columns], (8, HALF)
            )
        alive_tile[:, low : low + HALF] = jnp.broadcast_to(
            jnp.where(domain_ref[:, columns] == atoms_at, 1.0, 0.0), (8, HALF)
        )
    for s in range(gain_ref.shape[0]):
        gain_tile[s] = jnp.broadcast_to(gain_ref[s : s + 1, :], (FEAT, FEAT)).T

    def alive_of(place):
        return jnp.concatenate([alive_tile[:, place]] * (FEAT // 8), axis=0)

    def gain_of(place, columns):
        species = jnp.broadcast_to(species_ref[:, columns], (FEAT, 128))
        gain = gain_tile[0]
        for s in range(1, gain_ref.shape[0]):
            gain = jnp.where(species == s, gain_tile[s], gain)
        return gain * alive_of(place)

    def prepare(block, carry):
        for base, low in ((near_base, 0), (far_base, HALF)):
            columns = tile_of(base + block * 128, 128, 128)
            place = tile_of(low + block * 128, 128, 128)
            keys = k_ref[columns, :].astype(F32).T * gain_of(place, columns)
            key_t[:, place] = keys.astype(BF16)
            query_t[:, place] = (q_ref[columns, :].astype(F32).T * alive_of(place)).astype(BF16)
            if low == 0:
                value_t[:, place] = v_ref[columns, :].astype(F32).T.astype(BF16)
                grad_t[:, place] = g_ref[columns, :].astype(F32).T.astype(BF16)
        return carry

    lax.fori_loop(0, HALF // 128, prepare, 0)

    def coef(u):
        return weight_ref[u] * mask_ref[u].astype(F32) * (1.0 / math.sqrt(FEAT * ATOMS))

    def rotate_to(x_ref, y_ref, u, p, columns, cosine, sine):
        lead = x_ref[p : p + 16, columns]
        trail = x_ref[p + 64 : p + 80, columns]
        y_ref[u, p : p + 16, columns] = lead * cosine - trail * sine
        y_ref[u, p + 64 : p + 80, columns] = lead * sine + trail * cosine

    def angles(dirs, at, columns):
        projected = (
            dirs[0, at] * pos_tile[0, :, columns]
            + dirs[1, at] * pos_tile[1, :, columns]
            + dirs[2, at] * pos_tile[2, :, columns]
        )
        for low_f in range(0, FREQS, 16):
            pairs = []
            for f in (low_f, low_f + 8):
                freq = jnp.concatenate([freq_tile[f : f + 8, :]] * (WIDTH // 128), axis=1)
                pairs.append(cos_sin_turns(projected * freq))
            cosine = jnp.concatenate([pairs[0][0], pairs[1][0]], axis=0).astype(BF16)
            sine = jnp.concatenate([pairs[0][1], pairs[1][1]], axis=0).astype(BF16)
            yield low_f, cosine, sine

    dirs_copy = pltpu.make_async_remote_copy(
        src_ref=dirs_send,
        dst_ref=dirs_recv,
        send_sem=dirs_sem.at[0],
        recv_sem=dirs_sem.at[1],
        device_id={"dirs": 1 - dirs_at},
        device_id_type=pl.DeviceIdType.MESH,
    )
    to_scalars = pltpu.make_async_copy(dirs_recv, far_dirs, dirs_sem.at[2])

    def state_step(i):
        for u in range(GROUP):
            if u == GROUP // 2:

                @pl.when(i == 0)
                def _():
                    pl.semaphore_wait(barrier, len(partners))
                    dirs_copy.start()

                @pl.when(i == STEPS - 1)
                def _():
                    dirs_copy.wait()
                    to_scalars.start()

                exchange(2 * i, range(0, 2 * STEPS, 2))
            at = i * GROUP + u
            for low in range(0, ATOMS, WIDTH):
                columns = pl.ds(low, WIDTH)
                for low_f, cosine, sine in angles(dirs_ref, at, columns):
                    if low < HALF:
                        cos_sin[at, 0, low_f : low_f + 16, columns] = cosine
                        cos_sin[at, 1, low_f : low_f + 16, columns] = sine
                    for p in (low_f, low_f + FREQS):
                        rotate_to(key_t, key_rot, u, p, columns, cosine, sine)
                        rotate_to(query_t, query_rot, u, p, columns, cosine, sine)
        for at_row, rotated, rows in ((0, key_rot, v_ref), (ROWS, query_rot, g_ref)):
            product = jnp.zeros((ROWS, FEAT), F32)
            for base, low in ((near_base, 0), (far_base, HALF)):
                product = product + jnp.dot(
                    rotated[:, :, low : low + HALF].reshape(ROWS, HALF),
                    rows[tile_of(base, HALF, HALF), :],
                    preferred_element_type=F32,
                )
            for u in range(GROUP):
                part[i, at_row + u * FEAT : at_row + (u + 1) * FEAT, :] = (
                    product[u * FEAT : (u + 1) * FEAT] * coef(i * GROUP + u)
                ).astype(BF16)

    def far_angles(at):
        for low in range(0, HALF, WIDTH):
            columns = pl.ds(low, WIDTH)
            for low_f, cosine, sine in angles(far_dirs, at, columns):
                cos_sin[DIRS + at, 0, low_f : low_f + 16, columns] = cosine
                cos_sin[DIRS + at, 1, low_f : low_f + 16, columns] = sine

    def output_step(i, far):
        low_at = far * HALF
        table_at = far * DIRS + i * GROUP
        for u in range(GROUP):
            for low in range(0, HALF, WIDTH):
                columns = pl.ds(low, WIDTH)
                place = pl.ds(low_at + low, WIDTH)
                for low_f in range(0, FREQS, 16):
                    cosine = cos_sin[table_at + u, 0, low_f : low_f + 16, columns]
                    sine = cos_sin[table_at + u, 1, low_f : low_f + 16, columns]
                    for p in (low_f, low_f + FREQS):
                        for x_ref, y_ref in ((key_t, key_rot), (query_t, query_rot)):
                            lead = x_ref[p : p + 16, columns]
                            trail = x_ref[p + 64 : p + 80, columns]
                            y_ref[u, p : p + 16, place] = lead * cosine - trail * sine
                            y_ref[u, p + 64 : p + 80, place] = lead * sine + trail * cosine
        owner = 1 - dirs_at if far else dirs_at
        forward = state[owner, i, :ROWS, :]
        backward = state[owner, i, ROWS:, :]
        contract = (((0,), (0,)), ((), ()))
        for matrix, rotated, rows_t, total, back in (
            (forward, query_rot, grad_t, att_acc, back_q),
            (backward, key_rot, value_t, gv_acc, back_k),
        ):
            back[far] = (
                jnp.dot(matrix, rows_t[...], preferred_element_type=F32)
                .astype(BF16)
                .reshape(GROUP, FEAT, HALF)
            )
            total[...] += lax.dot_general(
                matrix,
                rotated[:, :, low_at : low_at + HALF].reshape(ROWS, HALF),
                contract,
                preferred_element_type=F32,
            )
        for low in range(0, HALF, WIDTH):
            columns = pl.ds(low, WIDTH)
            for low_f in range(0, FREQS, 16):
                tables = [
                    cos_sin[table_at + u, :, low_f : low_f + 16, columns] for u in range(GROUP)
                ]
                for p in (low_f, low_f + FREQS):
                    for back, total in ((back_q, gq_acc), (back_k, gk_acc)):
                        lead_sum = trail_sum = None
                        for u in range(GROUP):
                            cosine, sine = tables[u][0], tables[u][1]
                            lead = back[far, u, p : p + 16, columns]
                            trail = back[far, u, p + 64 : p + 80, columns]
                            new_lead = lead * cosine + trail * sine
                            new_trail = trail * cosine - lead * sine
                            lead_sum = new_lead if u == 0 else lead_sum + new_lead
                            trail_sum = new_trail if u == 0 else trail_sum + new_trail
                        total[p : p + 16, columns] += lead_sum.astype(F32)
                        total[p + 64 : p + 80, columns] += trail_sum.astype(F32)

    totals = (att_acc, gq_acc, gk_acc, gv_acc)
    for total in totals:
        total[...] = jnp.zeros_like(total)

    def first_loop(i, carry):
        state_step(i)
        exchange(2 * i + 1, range(1, 2 * STEPS, 2))
        return carry

    lax.fori_loop(0, STEPS, first_loop, 0)

    to_scalars.wait()

    def fill_loop(t, carry):
        exchange(t + 2 * STEPS, range(2 * STEPS, 2 * STEPS + FILL))

        def fill(n, inner):
            far_angles(t * (DIRS // FILL) + n)
            return inner

        return lax.fori_loop(0, DIRS // FILL, fill, carry)

    lax.fori_loop(0, FILL, fill_loop, 0)

    def second_loop(i, carry):
        at = 2 * STEPS + FILL
        for far in range(2):
            exchange(at + 2 * i + far, range(at + far, at + 2 * STEPS, 2))
            output_step(i, far)
        return carry

    lax.fori_loop(0, STEPS, second_loop, 0)

    def finish(block, carry):
        place = tile_of(block * 128, 128, 128)
        alive = alive_of(place)
        gain = gain_of(place, tile_of(near_base + block * 128, 128, 128))
        for total, out, factor in zip(
            totals, (att_out, gq_out, gk_out, gv_out), (None, alive, gain, None)
        ):
            whole = total[:, place]
            if factor is not None:
                whole = whole * factor
            out[:, place] = whole.astype(BF16)
        return carry

    lax.fori_loop(0, HALF // 128, finish, 0)


def turn_kernel(*refs):
    def turn(block, carry):
        rows = tile_of(block * 128, 128, 128)
        for source, result in zip(refs[:4], refs[4:]):
            result[rows, :] = source[:, rows].T
        return carry

    lax.fori_loop(0, HALF // 128, turn, 0)


def per_device(
    queries,
    keys,
    values,
    cotangent,
    positions,
    species,
    domain,
    species_gain,
    frequency,
    directions,
    dir_weight,
    dir_mask,
):
    smem = pl.BlockSpec(memory_space=pltpu.SMEM)
    vmem = pl.BlockSpec(memory_space=pltpu.VMEM)
    species_count = species_gain.shape[0]
    scratch = [
        pltpu.VMEM((FREQS, 128), F32),
        pltpu.VMEM((3, 8, ATOMS), F32),
        pltpu.VMEM((species_count, FEAT, FEAT), F32),
        pltpu.VMEM((8, ATOMS), F32),
        pltpu.VMEM((FEAT, ATOMS), BF16),
        pltpu.VMEM((FEAT, ATOMS), BF16),
        pltpu.VMEM((FEAT, HALF), BF16),
        pltpu.VMEM((FEAT, HALF), BF16),
        pltpu.VMEM((2 * DIRS, 2, FREQS, HALF), BF16),
        pltpu.VMEM((GROUP, FEAT, ATOMS), BF16),
        pltpu.VMEM((GROUP, FEAT, ATOMS), BF16),
        pltpu.VMEM((2, GROUP, FEAT, HALF), BF16),
        pltpu.VMEM((2, GROUP, FEAT, HALF), BF16),
        pltpu.VMEM((FEAT, HALF), F32),
        pltpu.VMEM((FEAT, HALF), F32),
        pltpu.VMEM((FEAT, HALF), F32),
        pltpu.VMEM((FEAT, HALF), F32),
        pltpu.VMEM((STEPS, 2 * ROWS, FEAT), BF16),
        pltpu.VMEM((STEPS, 2 * ROWS, FEAT), BF16),
        pltpu.VMEM((STEPS, 2 * ROWS, FEAT), BF16),
        pltpu.VMEM((2, STEPS, 2 * ROWS, FEAT), BF16),
        pltpu.VMEM((8, 128), F32),
        pltpu.VMEM((8, 128), F32),
        pltpu.SMEM((8, 128), F32),
        pltpu.SemaphoreType.DMA((STEPS, STAGES - 1)),
        pltpu.SemaphoreType.DMA((STEPS, STAGES - 1)),
        pltpu.SemaphoreType.DMA((3,)),
    ]
    turned = pl.pallas_call(
        kernel,
        out_shape=[jax.ShapeDtypeStruct((FEAT, HALF), BF16)] * 4,
        in_specs=[smem] * 4 + [vmem] * 9,
        out_specs=[vmem] * 4,
        scratch_shapes=scratch,
        compiler_params=pltpu.CompilerParams(
            collective_id=0, has_side_effects=True, vmem_limit_bytes=56 * 2**20
        ),
        name="fast_attention",
    )(
        frequency,
        directions,
        dir_weight,
        dir_mask,
        directions,
        queries,
        keys,
        values,
        cotangent,
        positions,
        species.reshape(1, ATOMS),
        domain.reshape(1, ATOMS),
        species_gain,
    )
    return tuple(
        pl.pallas_call(
            turn_kernel,
            out_shape=[jax.ShapeDtypeStruct((HALF, FEAT), BF16)] * 4,
            in_specs=[vmem] * 4,
            out_specs=[vmem] * 4,
            name="turn_results",
        )(*turned)
    )


def solution(mesh):
    return jax.shard_map(
        per_device,
        mesh=mesh,
        in_specs=(
            P("atoms", None),
            P("atoms", None),
            P("atoms", None),
            P("atoms", None),
            P(None, "atoms"),
            P("atoms"),
            P("atoms"),
            P(),
            P(),
            P(None, "dirs"),
            P("dirs"),
            P("dirs"),
        ),
        out_specs=(
            P(("atoms", "dirs"), None),
            P(("atoms", "dirs"), None),
            P(("atoms", "dirs"), None),
            P(("atoms", "dirs"), None),
        ),
        check_vma=False,
    )
```
